512 devices in a mesh: dp: 32 (over y, z_lo), ctx: 16 (over x, z_hi, core).
Axes of the slice: x: 4, y: 4, z: 16 (z_hi: 2, z_lo: 8; z = z_hi * 8 + z_lo), core: 2. Of those that a mesh axis runs over, the one named last changes fastest.
Arguments:
- projected: bfloat16 [65536, 2048], P(('dp', 'ctx')), may hold values from -6 to 6
- destination: int32 [16, 4096], P('ctx'), may hold values from 0 to 4095, as said below
- lengths: int32 [32, 3], P('dp'), may hold values from 1 to 1088, 1730 in all within a row
- grad_out: bfloat16 [65536, 512], P(('dp', 'ctx')), may hold values from -6 to 6
Outputs:
- layer_output: bfloat16 [65536, 512], P(('dp', 'ctx'))
- grad_projected: bfloat16 [65536, 2048], P(('dp', 'ctx'))
The draws below stay inside these ranges and needn't reach their ends.
Inputs may be any that keep to these rules, and one draw needn't show every extreme that they name: `destination`: row c maps the loader rows of ctx index c: entry i * 128 + r is m when row r of loader dp index i becomes row m % 128 of owner dp index m // 128. Each row is a permutation of 0 to 4095. From each loader device at most 8 rows go to one owner device, and exactly 8 to one of them. Row g holds the lengths of the 3 users of group g in packing order; they sum to 1730, and the longest is exactly 1088.
All inputs are finite; a program needn't handle non-finite values.
Results may differ from the reference program's by a relative error of at most 0.0085.
Values may be sent and summed in bfloat16 or wider, within the bound.
No kernel may reach another device: no remote copies, remote signals or barrier semaphores. Data moves between devices by JAX's collectives and lax.ppermute only.
A program may use at most 64 MiB of HBM per device.

```python
import math
import jax
import jax.numpy as jnp
import numpy as np
from jax import lax

HEADS = 4
HEAD_DIM = 128
BLOCK = 128
USERS = 3
WIDTH = 512
ROWS_DEV = 128
GROUP_ROWS = 2048
COLUMN_ROWS = 4096
TOTAL_ROWS = 65536
CAP = 8
MOST = 1088
TOTAL_LEN = 1730
N_DP = 32
N_CTX = 16


def route_column(key):
    subkeys = jax.random.split(key, 4)
    rotation = jax.random.randint(subkeys[0], (), 0, N_DP)
    shuffle = jax.random.permutation(subkeys[1], N_DP - 1)
    spread = jax.vmap(lambda part_key: jax.random.permutation(part_key, ROWS_DEV))(jax.random.split(subkeys[2], N_DP))
    settle = jax.vmap(lambda part_key: jax.random.permutation(part_key, ROWS_DEV))(jax.random.split(subkeys[3], N_DP))
    serial = jnp.arange(ROWS_DEV, dtype=jnp.int32)
    homeward = serial < CAP
    remain = jnp.maximum(serial - CAP, 0)
    offset = jnp.where(homeward, 0, 1 + shuffle[remain % (N_DP - 1)]).astype(jnp.int32)
    within = jnp.where(homeward, serial, remain // (N_DP - 1)).astype(jnp.int32)
    counts = jnp.sum((offset[:, None] == jnp.arange(N_DP, dtype=jnp.int32)[None, :]).astype(jnp.int32), axis=0)
    before = (jnp.cumsum(counts) - counts).astype(jnp.int32)
    position = before[offset] + within
    sources = jnp.broadcast_to(jnp.arange(N_DP, dtype=jnp.int32)[:, None], (N_DP, ROWS_DEV))
    owners = (sources + offset[None, :] + rotation) % N_DP
    position_grid = jnp.broadcast_to(position[None, :], (N_DP, ROWS_DEV))
    target = owners * ROWS_DEV + settle[owners, position_grid]
    mapping = jnp.zeros((N_DP, ROWS_DEV), jnp.int32).at[sources, spread].set(target.astype(jnp.int32))
    return mapping.reshape(N_DP * ROWS_DEV)


def draw_destination(key, part):
    key = jax.random.fold_in(key, 11)
    return jax.vmap(lambda column: route_column(jax.random.fold_in(key, column)))(jnp.arange(N_CTX, dtype=jnp.int32))


def level_of(stream_key, extent, cuts, smallest, largest):
    factor_of, own = 1.0, jax.random.fold_in(stream_key, 6)
    for dim, parts in cuts:
        heights = jnp.exp(jax.random.uniform(jax.random.fold_in(own, dim), (parts,), jnp.float32, smallest / len(cuts), largest / len(cuts)))
        factor_of = factor_of * jnp.repeat(heights, extent[dim] // parts).reshape([-1 if axis == dim else 1 for axis in range(len(extent))])
    return factor_of


def length_profile(count, total, limit, slope):
    portions = [(1 << 20) // math.isqrt(standing ** slope) + 1 for standing in range(2, count + 1)]
    rest, given = total - limit - (count - 1), [1] * (count - 1)
    while rest > 0:
        movable = [i for i in range(count - 1) if given[i] < limit]
        mass, left = sum([portions[i] for i in movable]), rest
        for i in movable:
            more = min(limit - given[i], max(1, left * portions[i] // mass), rest)
            given[i] = given[i] + more
            rest = rest - more
    return np.array([limit] + given)


def uneven_parts(key, number_of, total, limit, lean):
    if number_of == 2:
        one = jax.random.randint(key, (), max(1, total - limit), min(limit, total - 1) + 1)
        return jnp.stack([one, total - one])
    sizes = jnp.asarray(length_profile(number_of, total, limit, lean), jnp.int32)
    pairs = (number_of - 1) // 2
    donor, taker = sizes[1:1 + 2 * pairs:2], sizes[2:2 + 2 * pairs:2]
    slack = jnp.minimum(donor - 1, limit - taker)
    moved = jax.random.randint(jax.random.fold_in(key, 1), (pairs,), 0, 1 << 20) % (slack + 1)
    sizes = sizes.at[1:1 + 2 * pairs:2].set(donor - moved).at[2:2 + 2 * pairs:2].set(taker + moved)
    return sizes[jax.random.permutation(jax.random.fold_in(key, 2), number_of)]


def scatter_about(rng, extent, width, most, cuts=(), kind=jnp.bfloat16):
    array = width * jax.random.normal(rng, extent, jnp.float32)
    if cuts:
        array = array * level_of(rng, extent, cuts, -0.22, 0.18)
    return jnp.clip(array, -most, most).astype(kind)


def setup_inputs(seed: int = 0) -> dict:
    streams_of = jax.random.split(jax.random.key(seed), 5)
    projected = scatter_about(streams_of[0], (TOTAL_ROWS, 4 * WIDTH), 1.0, 6.0, ((0, 512),))
    destination = draw_destination(jax.random.fold_in(streams_of[4], 71), 0)
    lengths = jax.vmap(lambda own: uneven_parts(own, USERS, TOTAL_LEN, MOST, 0))(jax.random.split(streams_of[2], N_DP)).reshape((N_DP, USERS)).astype(jnp.int32)
    grad_out = scatter_about(streams_of[3], (TOTAL_ROWS, WIDTH), 1.0, 6.0, ((0, 512),))
    return dict(projected=projected, destination=destination, lengths=lengths, grad_out=grad_out)


EPSILON = 1e-06

def user_layout(positions, lengths_row):
    padded = (lengths_row + BLOCK - 1) // BLOCK * BLOCK
    starts = (jnp.cumsum(padded) - padded).astype(jnp.int32)
    ends = (starts + lengths_row).astype(jnp.int32)
    inside = (positions[:, None] >= starts[None, :]) & (positions[:, None] < ends[None, :])
    active = jnp.any(inside, axis=1)
    user_ids = lax.optimization_barrier(jnp.sum(jnp.where(inside, jnp.arange(USERS, dtype=jnp.int32)[None, :], 0), axis=1)).astype(jnp.int32)
    return (user_ids, active)

def pair_mask(query_pos, query_user, query_live, key_pos, key_user, key_live):
    allowed = (query_user[:, None] == key_user[None, :]) & query_live[:, None] & key_live[None, :]
    allowed = allowed & (key_pos[None, :] <= query_pos[:, None])
    return allowed.astype(jnp.float32)

def one_group(rows_in, cotangent, lengths_row):
    model_width = HEADS * HEAD_DIM
    score_scale = HEAD_DIM ** (-0.5)
    blocks = [rows_in[:, i * model_width:(i + 1) * model_width].astype(jnp.float32).reshape(GROUP_ROWS, HEADS, HEAD_DIM) for i in range(4)]
    gating, values, queries, key_rows = blocks
    positions = jnp.arange(GROUP_ROWS, dtype=jnp.int32)
    user_ids, active = user_layout(positions, lengths_row)
    allowed = pair_mask(positions, user_ids, active, positions, user_ids, active)
    scores = jnp.einsum('qhd,khd->hqk', queries, key_rows) * score_scale
    weights = (jax.nn.silu(scores) * allowed[None]).astype(jnp.bfloat16)
    mixed_sum = jnp.einsum('hqk,khd->qhd', weights.astype(jnp.float32), values)
    center = mixed_sum - lax.optimization_barrier(jnp.mean(mixed_sum, axis=-1, keepdims=True))
    inverse = lax.rsqrt(lax.optimization_barrier(jnp.mean(center * center, axis=-1, keepdims=True)) + EPSILON)
    normed = center * inverse
    layer_output = (normed * gating).astype(jnp.bfloat16).reshape(GROUP_ROWS, model_width)
    upstream = cotangent.astype(jnp.float32).reshape(GROUP_ROWS, HEADS, HEAD_DIM)
    grad_gating = upstream * normed
    grad_normed = upstream * gating
    grad_mixed = (grad_normed - lax.optimization_barrier(jnp.mean(grad_normed, axis=-1, keepdims=True)) - normed * lax.optimization_barrier(jnp.mean(grad_normed * normed, axis=-1, keepdims=True))) * inverse
    grad_mixed = grad_mixed.astype(jnp.bfloat16).astype(jnp.float32)
    grad_values = jnp.einsum('hqk,qhd->khd', weights.astype(jnp.float32), grad_mixed)
    grad_weights = jnp.einsum('qhd,khd->hqk', grad_mixed, values)
    sigmoid_part = jax.nn.sigmoid(scores)
    grad_scores = (grad_weights * allowed[None] * sigmoid_part * (1.0 + scores * (1.0 - sigmoid_part))).astype(jnp.bfloat16)
    grad_scores = grad_scores.astype(jnp.float32)
    grad_queries = jnp.einsum('hqk,khd->qhd', grad_scores, key_rows) * score_scale
    grad_keys = jnp.einsum('hqk,qhd->khd', grad_scores, queries) * score_scale
    gradients = jnp.concatenate([part.reshape(GROUP_ROWS, model_width) for part in (grad_gating, grad_values, grad_queries, grad_keys)], axis=1)
    return (layer_output, gradients.astype(jnp.bfloat16))

def reference(projected, destination, lengths, grad_out):
    model_width = HEADS * HEAD_DIM
    features = 4 * model_width
    loader = projected.reshape(N_DP, N_CTX, ROWS_DEV, features).transpose(1, 0, 2, 3).reshape(N_CTX, COLUMN_ROWS, features)
    owners = jax.vmap(lambda rows_in, mapping: jnp.zeros_like(rows_in).at[mapping].set(rows_in))(loader, destination)
    grouped = owners.reshape(N_CTX, N_DP, ROWS_DEV, features).transpose(1, 0, 2, 3).reshape(N_DP, GROUP_ROWS, features)
    cotangents = grad_out.reshape(N_DP, GROUP_ROWS, model_width)
    layer_output, gradients = lax.map(lambda group_items: one_group(*group_items), (grouped, cotangents, lengths))
    returned = gradients.reshape(N_DP, N_CTX, ROWS_DEV, features).transpose(1, 0, 2, 3).reshape(N_CTX, COLUMN_ROWS, features)
    restored = jax.vmap(lambda rows_in, mapping: rows_in[mapping])(returned, destination)
    restored = restored.reshape(N_CTX, N_DP, ROWS_DEV, features).transpose(1, 0, 2, 3).reshape(TOTAL_ROWS, features)
    return (layer_output.reshape(TOTAL_ROWS, model_width), restored)
```

```python
import functools

import jax
import jax.numpy as jnp
from jax import lax
from jax.experimental import pallas as pl
from jax.experimental.pallas import tpu as pltpu
from jax.sharding import Mesh
from jax.sharding import PartitionSpec as P

HEADS = 4
HEAD_DIM = 128
BLOCK = 128
USERS = 3
EPSILON = 1e-06
SCALE = HEAD_DIM ** (-0.5)
ROWS = 128
CAP = 8
N_DP = 32
N_X = 4
REACH = 2
PART = HEADS * ROWS
GROUP = N_X * PART
STEP = 256
VMEM_LIMIT = 48 * 1024 * 1024
CHUNK = 2 * CAP

F32 = jnp.float32
BF16 = jnp.bfloat16


def dot_nn(a, b):
    return lax.dot_general(a, b, (((1,), (0,)), ((), ())), preferred_element_type=F32)


def dot_nt(a, b):
    return lax.dot_general(a, b, (((1,), (1,)), ((), ())), preferred_element_type=F32)


def iota(shape, dim):
    return lax.broadcasted_iota(jnp.int32, shape, dim)


def call(kernel, outs, ins, smem, scratch=(), flops=0, nbytes=0):
    specs = [
        pl.BlockSpec(memory_space=pltpu.SMEM if s else pltpu.VMEM) for s in smem
    ]
    return pl.pallas_call(
        kernel,
        out_shape=outs,
        in_specs=specs,
        out_specs=[pl.BlockSpec(memory_space=pltpu.VMEM)] * len(outs),
        scratch_shapes=list(scratch),
        compiler_params=pltpu.CompilerParams(vmem_limit_bytes=VMEM_LIMIT),
        cost_estimate=pl.CostEstimate(flops=flops, bytes_accessed=nbytes, transcendentals=0),
    )(*ins)


def shape(*dims, dtype=BF16):
    return jax.ShapeDtypeStruct(dims, dtype)


def owners_of(dest_ref, dp):
    targets = dest_ref[pl.ds(dp, 1), :]
    owners = lax.shift_right_logical(targets, 7).astype(F32)
    across = jnp.broadcast_to(owners, (ROWS, ROWS))
    return across, across.T


def pack_kernel(ids_ref, dest_ref, proj_ref, out_ref):
    across, down = owners_of(dest_ref, ids_ref[0])
    square = (ROWS, ROWS)
    earlier = (across == down) & (iota(square, 0) < iota(square, 1))
    slot = jnp.sum(jnp.where(earlier, 1.0, 0.0), axis=0, keepdims=True)
    key = (across[0:1] * CAP + slot).astype(jnp.int32)
    pick = jnp.where(iota((N_DP * CAP, ROWS), 0) == key, 1.0, 0.0).astype(BF16)
    for j in range(2):
        for pair in range(0, HEADS, 2):
            halves = []
            for block in (j, 2 + j):
                at = (block * HEADS + pair) * HEAD_DIM
                moved = dot_nn(pick, proj_ref[:, at : at + 2 * HEAD_DIM])
                halves.append(moved.reshape(N_DP, CAP, 2 * HEAD_DIM))
            chunks = jnp.concatenate(halves, axis=1).astype(BF16)
            for h in range(2):
                out_ref[:, pair + h, :, j * HEAD_DIM : (j + 1) * HEAD_DIM] = chunks[
                    :, :, h * HEAD_DIM : (h + 1) * HEAD_DIM
                ]


def head_columns(h):
    return pl.ds(pl.multiple_of(h * HEAD_DIM, HEAD_DIM), HEAD_DIM)


def block_rows(c):
    return pl.ds(pl.multiple_of(c * ROWS, ROWS), ROWS)


def side_kernel(ids_ref, dest_ref, grad_ref, *out_refs):
    group = ids_ref[0]
    mapping = dest_ref[...]
    landing = lax.shift_right_logical(mapping, 7) == group
    landing_f = jnp.where(landing, 1.0, 0.0)
    square = (ROWS, ROWS)
    before = jnp.where(iota(square, 0) < iota(square, 1), 1.0, 0.0).astype(BF16)
    slot = dot_nn(landing_f.astype(BF16), before)
    code = iota((N_DP, ROWS), 0).astype(F32) * CAP + slot
    place = jnp.where(landing, mapping & (ROWS - 1), ROWS)
    row_of = iota(square, 0)
    total = jnp.zeros(square, F32)
    for i in range(N_DP):
        total = total + jnp.where(row_of == place[i : i + 1], code[i : i + 1], 0.0)
    codes = jnp.broadcast_to(jnp.sum(total, axis=1, keepdims=True), square).T
    for k, out_ref in enumerate(out_refs):
        out_ref[:ROWS] = grad_ref[:, head_columns(ids_ref[2] ^ k)]
        out_ref[ROWS:] = codes[:CHUNK].astype(BF16)


def chunk_row(code, half):
    return (code >> 3) * CHUNK + half * CAP + (code & (CAP - 1))


def code_across(side_ref):
    return side_ref[ROWS : ROWS + CHUNK].astype(F32)[0:1]


def both_halves(code, axis):
    return jnp.concatenate([chunk_row(code, half) for half in range(2)], axis=axis)


def pick_down(code):
    lane = iota((2 * ROWS, N_DP * CHUNK), 1)
    return jnp.where(lane == both_halves(code, 0), 1.0, 0.0).astype(BF16)


def unpack_kernel(
    ids_ref, s0, s1, s2, s3, arrived_ref, gate_ref, query_ref, vk_ref,
):
    for k, side_ref in enumerate((s0, s1, s2, s3)):
        c = ids_ref[2] ^ k
        rows = block_rows(c)
        chunks = arrived_ref[:, c].reshape(N_DP * CHUNK, 2 * HEAD_DIM)
        code = jnp.broadcast_to(code_across(side_ref), (ROWS, ROWS)).T.astype(jnp.int32)
        moved = dot_nn(pick_down(code[:, 0:1]), chunks).astype(BF16)
        gate_ref[rows] = moved[:ROWS, :HEAD_DIM]
        vk_ref[rows, :HEAD_DIM] = moved[:ROWS, HEAD_DIM:]
        query_ref[rows] = moved[ROWS:, :HEAD_DIM]
        vk_ref[rows, HEAD_DIM:] = moved[ROWS:, HEAD_DIM:]


def user_bounds(lengths_ref):
    bounds, start = [], jnp.int32(0)
    for u in range(USERS):
        length = lengths_ref[0, u]
        padded = (length + BLOCK - 1) // BLOCK * BLOCK
        bounds.append((start, start + length, start + padded))
        start = start + padded
    return bounds


def first_key(positions, bounds):
    low = jnp.full(positions.shape, 2 * GROUP, jnp.int32)
    for start, end, _ in bounds:
        low = jnp.where((positions >= start) & (positions < end), start, low)
    return low


def half_scores(a, b):
    return dot_nt(a, b) * (0.5 * SCALE)


def silu_of(half, tanh):
    return half + half * tanh


def slope_of(half, tanh):
    return (0.5 + 0.5 * tanh) * (1.0 + half * (1.0 - tanh))


def key_steps(base, bounds):
    lowest = jnp.int32(0)
    for start, _, _ in bounds:
        lowest = jnp.where(start <= base, start, lowest)
    return lowest // STEP, (base + PART) // STEP


def gather_parts(held, parts):
    for n, part in enumerate(parts):
        held[n * PART : (n + 1) * PART] = part[...]


def forward_kernel(
    ids_ref, lengths_ref, s0, s1, s2, s3, gate_ref, query_ref, vk2_ref, vk1_ref, vk0_ref,
    mixed_ref, gate_grad_ref, l0, l1, l2, l3, held,
):
    gather_parts(held, (vk2_ref, vk1_ref, vk0_ref))
    bounds = user_bounds(lengths_ref)
    base = ids_ref[1] * PART
    first_step, last_step = key_steps(base, bounds)
    query_pos = base + iota((PART, 1), 0)
    low = first_key(query_pos, bounds)
    queries = query_ref[...]

    def step(k, total):
        at = k * STEP
        rows = pl.ds(pl.multiple_of(at - base + REACH * PART, STEP), STEP)
        values = held[rows, :HEAD_DIM]
        keys = held[rows, HEAD_DIM:]
        half = half_scores(queries, keys)
        key_pos = at + iota((1, STEP), 1)
        allowed = (key_pos >= low) & (key_pos <= query_pos)
        weights = jnp.where(allowed, silu_of(half, jnp.tanh(half)), 0.0).astype(BF16)
        return total + dot_nn(weights, values)

    mixed_sum = lax.fori_loop(first_step, last_step, step, jnp.zeros((PART, HEAD_DIM), F32))
    center = mixed_sum - jnp.mean(mixed_sum, axis=-1, keepdims=True)
    inverse = lax.rsqrt(jnp.mean(center * center, axis=-1, keepdims=True) + EPSILON)
    normed = center * inverse
    gating = gate_ref[...].astype(F32)
    head = ids_ref[2]
    for k, part in enumerate((s0, s1, s2, s3)):
        held[block_rows(head ^ k), HEAD_DIM:] = part[:ROWS]
    upstream = held[:PART, HEAD_DIM:].astype(F32)
    layer = (normed * gating).astype(BF16)
    grad_normed = upstream * gating
    mixed_ref[...] = (
        (
            grad_normed
            - jnp.mean(grad_normed, axis=-1, keepdims=True)
            - normed * jnp.mean(grad_normed * normed, axis=-1, keepdims=True)
        )
        * inverse
    ).astype(BF16)
    gate_grad_ref[...] = (upstream * normed).astype(BF16)
    held[:PART, :HEAD_DIM] = layer
    for k, layer_ref in enumerate((l0, l1, l2, l3)):
        layer_ref[...] = held[block_rows(head ^ k), :HEAD_DIM]


def query_steps(base, bounds):
    highest = bounds[-1][2]
    for start, _, _ in reversed(bounds):
        highest = jnp.where(start >= base + PART, start, highest)
    return base // STEP, (highest + STEP - 1) // STEP


def query_grad_kernel(
    ids_ref, lengths_ref, s0, s1, s2, s3, mixed_ref, gate_grad_ref, q0_ref, q1_ref, q2_ref,
    vk2_ref, vk1_ref, vk0_ref, out_ref, weights_ref, slope_ref, held, held_q, done,
):
    gather_parts(held, (vk2_ref, vk1_ref, vk0_ref))
    gather_parts(held_q, (q0_ref, q1_ref, q2_ref))
    bounds = user_bounds(lengths_ref)
    base = ids_ref[1] * PART
    own_pos = base + iota((PART, 1), 0)
    low = first_key(own_pos, bounds)
    queries = q0_ref[...]
    grad_mixed = mixed_ref[...]

    def step(k, total):
        at = k * STEP
        rows = pl.ds(pl.multiple_of(at - base + REACH * PART, STEP), STEP)
        values = held[rows, :HEAD_DIM]
        keys = held[rows, HEAD_DIM:]
        half = half_scores(queries, keys)
        key_pos = at + iota((1, STEP), 1)
        allowed = (key_pos >= low) & (key_pos <= own_pos)
        slope = jnp.where(allowed, slope_of(half, jnp.tanh(half)), 0.0)
        grad_scores = (dot_nt(grad_mixed, values) * slope).astype(BF16)
        return total + dot_nn(grad_scores, keys)

    total = lax.fori_loop(*key_steps(base, bounds), step, jnp.zeros((PART, HEAD_DIM), F32))
    done[0] = gate_grad_ref[...]
    done[1] = (total * SCALE).astype(BF16)
    pack_back(ids_ref, (s0, s1, s2, s3), done, out_ref, 0)
    own_keys = vk0_ref[:, HEAD_DIM:]

    def key_step(k, carry):
        at = k * STEP
        n = k - base // STEP
        query_pos = at + iota((1, STEP), 1)
        first = first_key(query_pos, bounds)
        half = half_scores(own_keys, held_q[pl.ds(pl.multiple_of(n * STEP, STEP), STEP)])
        allowed = (own_pos >= first) & (own_pos <= query_pos)
        tanh = jnp.tanh(half)
        weights_ref[n] = jnp.where(allowed, silu_of(half, tanh), 0.0).astype(BF16)
        slope_ref[n] = jnp.where(allowed, slope_of(half, tanh), 0.0)
        return carry

    lax.fori_loop(*query_steps(base, bounds), key_step, 0)


def pack_back(ids_ref, sides, done, out_ref, j):
    sublane = iota((N_DP * CHUNK, 2 * ROWS), 0)
    for k, side_ref in enumerate(sides):
        c = ids_ref[2] ^ k
        at = both_halves(code_across(side_ref).astype(jnp.int32), 1)
        pick = jnp.where(sublane == at, 1.0, 0.0).astype(BF16)
        rows = jnp.concatenate([done[0, block_rows(c)], done[1, block_rows(c)]], axis=0)
        out_ref[:, c, :, j * HEAD_DIM : (j + 1) * HEAD_DIM] = (
            dot_nn(pick, rows).astype(BF16).reshape(N_DP, CHUNK, HEAD_DIM)
        )


def backward_kernel(
    ids_ref, lengths_ref, s0, s1, s2, s3, vk_ref, q0_ref, q1_ref, q2_ref,
    m0_ref, m1_ref, m2_ref, weights_ref, slope_ref, gq_ref, out_ref, held_q, held_m, done,
):
    gather_parts(held_q, (q0_ref, q1_ref, q2_ref))
    gather_parts(held_m, (m0_ref, m1_ref, m2_ref))
    out_ref[:, :, :, :HEAD_DIM] = gq_ref[...]
    bounds = user_bounds(lengths_ref)
    base = ids_ref[1] * PART
    values = vk_ref[:, :HEAD_DIM]

    def step(k, totals):
        grad_values, grad_keys = totals
        n = k - base // STEP
        rows = pl.ds(pl.multiple_of(n * STEP, STEP), STEP)
        grad_mixed = held_m[rows]
        grad_scores = (dot_nt(values, grad_mixed) * slope_ref[n]).astype(BF16)
        return (
            grad_values + dot_nn(weights_ref[n], grad_mixed),
            grad_keys + dot_nn(grad_scores, held_q[rows]),
        )

    zeros = jnp.zeros((PART, HEAD_DIM), F32)
    grad_values, grad_keys = lax.fori_loop(*query_steps(base, bounds), step, (zeros, zeros))
    done[0] = grad_values.astype(BF16)
    done[1] = (grad_keys * SCALE).astype(BF16)
    pack_back(ids_ref, (s0, s1, s2, s3), done, out_ref, 1)


def finish_kernel(ids_ref, dest_ref, l0, l1, l2, l3, back_ref, grad_ref, out_ref):
    across, down = owners_of(dest_ref, ids_ref[0])
    square = (ROWS, ROWS)
    earlier = (across == down) & (iota(square, 1) < iota(square, 0))
    slot = jnp.sum(jnp.where(earlier, 1.0, 0.0), axis=1, keepdims=True)
    code = (down[:, 0:1] * CAP + slot).astype(jnp.int32)
    pick = pick_down(code)
    for k, layer_ref in enumerate((l0, l1, l2, l3)):
        out_ref[:, head_columns(ids_ref[2] ^ k)] = layer_ref[...]
    for h in range(HEADS):
        chunks = back_ref[:, h].reshape(N_DP * CHUNK, 2 * HEAD_DIM)
        moved = dot_nn(pick, chunks).astype(BF16)
        for half in range(2):
            for j in range(2):
                at = ((2 * half + j) * HEADS + h) * HEAD_DIM
                grad_ref[:, at : at + HEAD_DIM] = moved[
                    half * ROWS : (half + 1) * ROWS, j * HEAD_DIM : (j + 1) * HEAD_DIM
                ]


def route(chunks):
    flat = chunks.reshape(N_DP * HEADS * CHUNK, 2 * HEAD_DIM)
    moved = lax.all_to_all(flat, ("dp", "h"), 0, 0, tiled=True)
    return moved.reshape(chunks.shape)


def from_quarter(array, by):
    pairs = [(i, i - by) for i in range(N_X) if 0 <= i - by < N_X]
    return lax.ppermute(array, "x", pairs)


def swap_heads(pieces):
    moved = [
        lax.ppermute(piece, "h", [(i, i ^ k) for i in range(HEADS)])
        for k, piece in enumerate(pieces)
        if k
    ]
    return [pieces[0], *moved]


def body(projected, destination, lengths, grad_out):
    ids = jnp.stack([lax.axis_index(axis) for axis in ("dp", "x", "h")]).astype(jnp.int32)
    mapping = destination.reshape(N_DP, ROWS)
    chunked = shape(N_DP, HEADS, CHUNK, 2 * HEAD_DIM)
    half_chunked = shape(N_DP, HEADS, CHUNK, HEAD_DIM)
    head_part = shape(PART, HEAD_DIM)
    pieces = [shape(ROWS, HEAD_DIM)] * HEADS
    (packed,) = call(
        pack_kernel, [chunked], (ids, mapping, projected), (1, 0, 0),
        flops=2 * 256 * 128 * 2048, nbytes=3 << 19,
    )
    side_out = call(
        side_kernel, [shape(ROWS + CHUNK, HEAD_DIM)] * HEADS, (ids, mapping, grad_out), (1, 0, 0),
        nbytes=3 << 17,
    )
    side = swap_heads(side_out)
    arrived = route(packed)
    gate, queries, vk = call(
        unpack_kernel, [head_part, head_part, shape(PART, 2 * HEAD_DIM)],
        (ids, *side, arrived), (1,) + (0,) * 5,
        flops=1 << 28, nbytes=2 << 20,
    )
    vk_parts = (from_quarter(vk, -2), from_quarter(vk, -1), vk)
    query_parts = (queries, from_quarter(queries, 1), from_quarter(queries, 2))
    span = (REACH + 1) * PART
    held_vk = pltpu.VMEM((span, 2 * HEAD_DIM), BF16)
    held_one = pltpu.VMEM((span, HEAD_DIM), BF16)
    done = pltpu.VMEM((2, PART, HEAD_DIM), BF16)
    mixed, gate_grad, *layer = call(
        forward_kernel, [head_part, head_part, *pieces],
        (ids, lengths, *side, gate, queries, *vk_parts), (1, 1) + (0,) * 9,
        scratch=[held_vk], flops=1 << 29, nbytes=2 << 20,
    )
    mixed_parts = (mixed, from_quarter(mixed, 1), from_quarter(mixed, 2))
    layer_home = swap_heads(layer)
    gq_back, weights, slopes = call(
        query_grad_kernel,
        [half_chunked, shape(span // STEP, PART, STEP), shape(span // STEP, PART, STEP, dtype=F32)],
        (ids, lengths, *side, mixed, gate_grad, *query_parts, *vk_parts), (1, 1) + (0,) * 12,
        scratch=[held_vk, held_one, done], flops=1 << 29, nbytes=2 << 20,
    )
    (back,) = call(
        backward_kernel, [chunked],
        (ids, lengths, *side, vk, *query_parts, *mixed_parts, weights, slopes, gq_back),
        (1, 1) + (0,) * 14,
        scratch=[held_one, held_one, done], flops=1 << 30, nbytes=3 << 20,
    )
    home = route(back)
    grad_projected, layer_output = call(
        finish_kernel, [shape(ROWS, 4 * HEADS * HEAD_DIM), shape(ROWS, HEADS * HEAD_DIM)],
        (ids, mapping, *layer_home, home), (1, 0, 0, 0, 0, 0, 0),
        flops=1 << 28, nbytes=2 << 20,
    )
    return (layer_output, grad_projected)


def solution(mesh):
    fine = Mesh(mesh.devices.reshape(N_DP, N_X, HEADS), ("dp", "x", "h"))
    rows = P(("dp", "x", "h"), None)
    in_specs = (rows, P(("x", "h"), None), P("dp", None), rows)
    return jax.shard_map(
        body, mesh=fine, in_specs=in_specs, out_specs=(rows, rows), check_vma=False
    )
```

```python
import functools

import jax
import jax.numpy as jnp
from jax import lax
from jax.experimental import pallas as pl
from jax.experimental.pallas import tpu as pltpu
from jax.sharding import Mesh
from jax.sharding import PartitionSpec as P

HEADS = 4
HEAD_DIM = 128
BLOCK = 128
USERS = 3
EPSILON = 1e-06
SCALE = HEAD_DIM ** (-0.5)
ROWS = 128
CAP = 8
N_DP = 32
N_X = 4
REACH = 2
PART = HEADS * ROWS
GROUP = N_X * PART
STEP = 256
VMEM_LIMIT = 48 * 1024 * 1024
CHUNK = 2 * CAP

F32 = jnp.float32
BF16 = jnp.bfloat16


def dot_nn(a, b):
    return lax.dot_general(a, b, (((1,), (0,)), ((), ())), preferred_element_type=F32)


def dot_nt(a, b):
    return lax.dot_general(a, b, (((1,), (1,)), ((), ())), preferred_element_type=F32)


def iota(shape, dim):
    return lax.broadcasted_iota(jnp.int32, shape, dim)


def call(kernel, outs, ins, smem, scratch=(), flops=0, nbytes=0, hbm_in=(), hbm_out=False, limit=VMEM_LIMIT):
    spaces = [pltpu.SMEM if s else pltpu.VMEM for s in smem]
    for n in hbm_in:
        spaces[n] = pl.ANY
    return pl.pallas_call(
        kernel,
        out_shape=outs,
        in_specs=[pl.BlockSpec(memory_space=space) for space in spaces],
        out_specs=[pl.BlockSpec(memory_space=pl.ANY if hbm_out else pltpu.VMEM)] * len(outs),
        scratch_shapes=list(scratch),
        compiler_params=pltpu.CompilerParams(vmem_limit_bytes=limit),
        name=kernel.__name__,
        cost_estimate=pl.CostEstimate(flops=flops, bytes_accessed=nbytes, transcendentals=0),
    )(*ins)


def shape(*dims, dtype=BF16):
    return jax.ShapeDtypeStruct(dims, dtype)


def owners_of(dest_ref, dp):
    targets = dest_ref[pl.ds(dp, 1), :]
    owners = lax.shift_right_logical(targets, 7).astype(F32)
    across = jnp.broadcast_to(owners, (ROWS, ROWS))
    return across, across.T


def pack_kernel(ids_ref, dest_ref, proj_ref, out_ref, proj, packed, in_sem, out_sems):
    load = pltpu.make_async_copy(proj_ref, proj, in_sem)
    load.start()
    across, down = owners_of(dest_ref, ids_ref[0])
    square = (ROWS, ROWS)
    earlier = (across == down) & (iota(square, 0) < iota(square, 1))
    slot = jnp.sum(jnp.where(earlier, 1.0, 0.0), axis=0, keepdims=True)
    key = (across[0:1] * CAP + slot).astype(jnp.int32)
    pick = jnp.where(iota((N_DP * CAP, ROWS), 0) == key, 1.0, 0.0).astype(BF16)
    load.wait()
    stores = []
    for pair in range(0, HEADS, 2):
        for j in range(2):
            halves = []
            for block in (j, 2 + j):
                at = (block * HEADS + pair) * HEAD_DIM
                moved = dot_nn(pick, proj[:, at : at + 2 * HEAD_DIM])
                halves.append(moved.reshape(N_DP, CAP, 2 * HEAD_DIM))
            chunks = jnp.concatenate(halves, axis=1).astype(BF16)
            for h in range(2):
                packed[:, pair + h, :, j * HEAD_DIM : (j + 1) * HEAD_DIM] = chunks[
                    :, :, h * HEAD_DIM : (h + 1) * HEAD_DIM
                ]
        heads = slice(pair, pair + 2)
        stores.append(
            pltpu.make_async_copy(packed.at[:, heads], out_ref.at[:, heads], out_sems.at[pair // 2])
        )
        stores[-1].start()
    for store in stores:
        store.wait()


def head_columns(h):
    return pl.ds(pl.multiple_of(h * HEAD_DIM, HEAD_DIM), HEAD_DIM)


def block_rows(c):
    return pl.ds(pl.multiple_of(c * ROWS, ROWS), ROWS)


def side_kernel(ids_ref, dest_ref, grad_ref, *out_refs):
    *out_refs, home_ref = out_refs
    across, down = owners_of(dest_ref, ids_ref[0])
    earlier = (across == down) & (iota((ROWS, ROWS), 1) < iota((ROWS, ROWS), 0))
    rank = jnp.sum(jnp.where(earlier, 1.0, 0.0), axis=1, keepdims=True)
    home_ref[...] = pick_down((down[:, 0:1] * CAP + rank).astype(jnp.int32))
    group = ids_ref[0]
    mapping = dest_ref[...]
    landing = lax.shift_right_logical(mapping, 7) == group
    landing_f = jnp.where(landing, 1.0, 0.0)
    square = (ROWS, ROWS)
    before = jnp.where(iota(square, 0) < iota(square, 1), 1.0, 0.0).astype(BF16)
    slot = dot_nn(landing_f.astype(BF16), before)
    code = iota((N_DP, ROWS), 0).astype(F32) * CAP + slot
    place = jnp.where(landing, mapping & (ROWS - 1), ROWS)
    row_of = iota(square, 0)
    total = jnp.zeros(square, F32)
    for i in range(N_DP):
        total = total + jnp.where(row_of == place[i : i + 1], code[i : i + 1], 0.0)
    codes = jnp.broadcast_to(jnp.sum(total, axis=1, keepdims=True), square).T
    for k, out_ref in enumerate(out_refs):
        out_ref[:ROWS] = grad_ref[:, head_columns(ids_ref[2] ^ k)]
        out_ref[ROWS:] = codes[:CHUNK].astype(BF16)


def chunk_row(code, half):
    return (code >> 3) * CHUNK + half * CAP + (code & (CAP - 1))


def code_across(side_ref):
    return side_ref[ROWS : ROWS + CHUNK].astype(F32)[0:1]


def both_halves(code, axis):
    return jnp.concatenate([chunk_row(code, half) for half in range(2)], axis=axis)


def pick_down(code):
    lane = iota((2 * ROWS, N_DP * CHUNK), 1)
    return jnp.where(lane == both_halves(code, 0), 1.0, 0.0).astype(BF16)


def unpack_kernel(
    ids_ref, s0, s1, s2, s3, arrived_ref, gate_ref, query_ref, vk_ref,
):
    for k, side_ref in enumerate((s0, s1, s2, s3)):
        c = ids_ref[2] ^ k
        rows = block_rows(c)
        chunks = arrived_ref[:, c].reshape(N_DP * CHUNK, 2 * HEAD_DIM)
        code = jnp.broadcast_to(code_across(side_ref), (ROWS, ROWS)).T.astype(jnp.int32)
        moved = dot_nn(pick_down(code[:, 0:1]), chunks).astype(BF16)
        gate_ref[rows] = moved[:ROWS, :HEAD_DIM]
        vk_ref[rows, :HEAD_DIM] = moved[:ROWS, HEAD_DIM:]
        query_ref[rows] = moved[ROWS:, :HEAD_DIM]
        vk_ref[rows, HEAD_DIM:] = moved[ROWS:, HEAD_DIM:]


def user_bounds(lengths_ref):
    bounds, start = [], jnp.int32(0)
    for u in range(USERS):
        length = lengths_ref[0, u]
        padded = (length + BLOCK - 1) // BLOCK * BLOCK
        bounds.append((start, start + length, start + padded))
        start = start + padded
    return bounds


def first_key(positions, bounds):
    low = jnp.full(positions.shape, 2 * GROUP, jnp.int32)
    for start, end, _ in bounds:
        low = jnp.where((positions >= start) & (positions < end), start, low)
    return low


def half_scores(a, b):
    return dot_nt(a, b) * (0.5 * SCALE)


def silu_of(half, tanh):
    return half + half * tanh


def slope_of(half, tanh):
    return (0.5 + 0.5 * tanh) * (1.0 + half * (1.0 - tanh))


def pairs_allowed(key_pos, query_pos, bounds):
    low = first_key(query_pos, bounds)
    return (key_pos >= low) & (key_pos <= query_pos)


def steps_of(parts, quarters):
    for part, quarter in zip(parts, quarters):
        for at in range(0, PART, STEP):
            yield part, slice(at, at + STEP), quarter * PART + at


def forward_kernel(
    ids_ref, lengths_ref, s0, s1, s2, s3, gate_ref, query_ref, vk1_ref, vk2_ref, vk0_ref,
    mixed_ref, gate_grad_ref, l0, l1, l2, l3, held,
):
    bounds = user_bounds(lengths_ref)
    quarter = ids_ref[1]
    query_pos = quarter * PART + iota((PART, 1), 0)
    queries = query_ref[...]
    mixed_sum = jnp.zeros((PART, HEAD_DIM), F32)
    for vk_ref, rows, at in steps_of(
        (vk2_ref, vk1_ref, vk0_ref), (quarter - 2, quarter - 1, quarter)
    ):
        half = half_scores(queries, vk_ref[rows, HEAD_DIM:])
        allowed = pairs_allowed(at + iota((1, STEP), 1), query_pos, bounds)
        weights = jnp.where(allowed, silu_of(half, jnp.tanh(half)), 0.0).astype(BF16)
        mixed_sum = mixed_sum + dot_nn(weights, vk_ref[rows, :HEAD_DIM])
    center = mixed_sum - jnp.mean(mixed_sum, axis=-1, keepdims=True)
    inverse = lax.rsqrt(jnp.mean(center * center, axis=-1, keepdims=True) + EPSILON)
    normed = center * inverse
    gating = gate_ref[...].astype(F32)
    head = ids_ref[2]
    for k, part in enumerate((s0, s1, s2, s3)):
        held[block_rows(head ^ k), HEAD_DIM:] = part[:ROWS]
    upstream = held[:, HEAD_DIM:].astype(F32)
    layer = (normed * gating).astype(BF16)
    grad_normed = upstream * gating
    mixed_ref[...] = (
        (
            grad_normed
            - jnp.mean(grad_normed, axis=-1, keepdims=True)
            - normed * jnp.mean(grad_normed * normed, axis=-1, keepdims=True)
        )
        * inverse
    ).astype(BF16)
    gate_grad_ref[...] = (upstream * normed).astype(BF16)
    held[:, :HEAD_DIM] = layer
    for k, layer_ref in enumerate((l0, l1, l2, l3)):
        layer_ref[...] = held[block_rows(head ^ k), :HEAD_DIM]


def key_grads(keys, values, key_pos, queries, grad_mixed, query_pos, bounds):
    half = half_scores(keys, queries)
    allowed = pairs_allowed(key_pos, query_pos, bounds)
    tanh = jnp.tanh(half)
    weights = jnp.where(allowed, silu_of(half, tanh), 0.0).astype(BF16)
    slope = jnp.where(allowed, slope_of(half, tanh), 0.0)
    grad_scores = (dot_nt(values, grad_mixed) * slope).astype(BF16)
    return dot_nn(weights, grad_mixed), dot_nn(grad_scores, queries)


def query_grad_kernel(
    ids_ref, lengths_ref, s0, s1, s2, s3, mixed_ref, gate_grad_ref, query_ref,
    vk1_ref, vk2_ref, vk0_ref, out_ref, own_ref, picks_ref, done,
):
    bounds = user_bounds(lengths_ref)
    quarter = ids_ref[1]
    own_pos = quarter * PART + iota((PART, 1), 0)
    queries = query_ref[...]
    grad_mixed = mixed_ref[...]
    total = jnp.zeros((PART, HEAD_DIM), F32)
    for vk_ref, rows, at in steps_of(
        (vk2_ref, vk1_ref, vk0_ref), (quarter - 2, quarter - 1, quarter)
    ):
        keys = vk_ref[rows, HEAD_DIM:]
        half = half_scores(queries, keys)
        allowed = pairs_allowed(at + iota((1, STEP), 1), own_pos, bounds)
        slope = jnp.where(allowed, slope_of(half, jnp.tanh(half)), 0.0)
        grad_scores = (dot_nt(grad_mixed, vk_ref[rows, :HEAD_DIM]) * slope).astype(BF16)
        total = total + dot_nn(grad_scores, keys)
    done[0] = gate_grad_ref[...]
    done[1] = (total * SCALE).astype(BF16)
    back_picks(ids_ref, (s0, s1, s2, s3), picks_ref)
    pack_back(picks_ref, done, out_ref, 0)
    values, keys = vk0_ref[:, :HEAD_DIM], vk0_ref[:, HEAD_DIM:]
    sums = (0.0, 0.0)
    for part, rows, at in steps_of((query_ref,), (quarter,)):
        terms = key_grads(
            keys, values, own_pos, part[rows], mixed_ref[rows], at + iota((1, STEP), 1), bounds
        )
        sums = tuple(a + b for a, b in zip(sums, terms))
    for n in range(2):
        own_ref[n] = sums[n]


def back_picks(ids_ref, sides, picks_ref):
    sublane = iota((N_DP * CHUNK, 2 * ROWS), 0)
    for k, side_ref in enumerate(sides):
        at = both_halves(code_across(side_ref).astype(jnp.int32), 1)
        picks_ref[ids_ref[2] ^ k] = jnp.where(sublane == at, 1.0, 0.0).astype(BF16)


def pack_back(picks_ref, done, out_ref, j, finished=lambda c: None):
    for c in range(HEADS):
        rows = slice(c * ROWS, (c + 1) * ROWS)
        both = jnp.concatenate([done[0, rows], done[1, rows]], axis=0)
        out_ref[:, c, :, j * HEAD_DIM : (j + 1) * HEAD_DIM] = (
            dot_nn(picks_ref[c], both).astype(BF16).reshape(N_DP, CHUNK, HEAD_DIM)
        )
        finished(c)


def backward_kernel(
    ids_ref, lengths_ref, picks_ref, vk_ref, q2_ref, q1_ref, m2_ref, m1_ref,
    own_ref, gq_ref, out_ref, done, packed, sems,
):
    packed[:, :, :, :HEAD_DIM] = gq_ref[...]
    bounds = user_bounds(lengths_ref)
    quarter = ids_ref[1]
    own_pos = quarter * PART + iota((PART, 1), 0)
    values, keys = vk_ref[:, :HEAD_DIM], vk_ref[:, HEAD_DIM:]
    sums = (own_ref[0], own_ref[1])
    for (part, mixed), rows, at in steps_of(
        ((q1_ref, m1_ref), (q2_ref, m2_ref)), (quarter + 1, quarter + 2)
    ):
        terms = key_grads(
            keys, values, own_pos, part[rows], mixed[rows], at + iota((1, STEP), 1), bounds
        )
        sums = tuple(a + b for a, b in zip(sums, terms))
    done[0] = sums[0].astype(BF16)
    done[1] = (sums[1] * SCALE).astype(BF16)
    stores = []

    def send(c):
        stores.append(pltpu.make_async_copy(packed.at[:, c], out_ref.at[:, c], sems.at[c]))
        stores[-1].start()

    pack_back(picks_ref, done, packed, 1, send)
    for store in stores:
        store.wait()


def finish_kernel(
    ids_ref, home_ref, l0, l1, l2, l3, back_ref, grad_ref, out_ref, grads, layer, sems
):
    head = ids_ref[2]
    for k, layer_ref in enumerate((l0, l1, l2, l3)):
        layer[:, head_columns(head ^ k)] = layer_ref[...]
    stores = [pltpu.make_async_copy(layer, out_ref, sems.at[HEADS])]
    stores[0].start()
    pick = home_ref[...]
    for h in range(HEADS):
        chunks = back_ref[:, h].reshape(N_DP * CHUNK, 2 * HEAD_DIM)
        moved = dot_nn(pick, chunks).astype(BF16)
        for half in range(2):
            for j in range(2):
                block = 2 * half + j
                at = (block * HEADS + h) * HEAD_DIM
                columns = slice(at, at + HEAD_DIM)
                grads[:, columns] = moved[
                    half * ROWS : (half + 1) * ROWS, j * HEAD_DIM : (j + 1) * HEAD_DIM
                ]
                stores.append(
                    pltpu.make_async_copy(
                        grads.at[:, columns], grad_ref.at[:, columns], sems.at[HEADS + 1 + 4 * h + block]
                    )
                )
                stores[-1].start()
    for store in stores:
        store.wait()


def route(chunks):
    flat = chunks.reshape(N_DP * HEADS * CHUNK, 2 * HEAD_DIM)
    moved = lax.all_to_all(flat, ("dp", "h"), 0, 0, tiled=True)
    return moved.reshape(chunks.shape)


def from_quarter(array, by):
    pairs = [(i, i - by) for i in range(N_X) if 0 <= i - by < N_X]
    return lax.ppermute(array, "x", pairs)


def swap_heads(pieces):
    moved = [
        lax.ppermute(piece, "h", [(i, i ^ k) for i in range(HEADS)])
        for k, piece in enumerate(pieces)
        if k
    ]
    return [pieces[0], *moved]


def body(projected, destination, lengths, grad_out):
    ids = jnp.stack([lax.axis_index(axis) for axis in ("dp", "x", "h")]).astype(jnp.int32)
    mapping = destination.reshape(N_DP, ROWS)
    chunked = shape(N_DP, HEADS, CHUNK, 2 * HEAD_DIM)
    half_chunked = shape(N_DP, HEADS, CHUNK, HEAD_DIM)
    head_part = shape(PART, HEAD_DIM)
    pieces = [shape(ROWS, HEAD_DIM)] * HEADS
    (packed,) = call(
        pack_kernel, [chunked], (ids, mapping, projected), (1, 0, 0),
        scratch=[
            pltpu.VMEM(projected.shape, BF16), pltpu.VMEM(chunked.shape, BF16),
            pltpu.SemaphoreType.DMA, pltpu.SemaphoreType.DMA((2,)),
        ],
        flops=2 * 256 * 128 * 2048, nbytes=3 << 19, hbm_in=(2,), hbm_out=True, limit=62 * 1024 * 1024,
    )
    *side_out, home = call(
        side_kernel, [shape(ROWS + CHUNK, HEAD_DIM)] * HEADS + [shape(2 * ROWS, N_DP * CHUNK)], (ids, mapping, grad_out), (1, 0, 0),
        nbytes=3 << 17,
    )
    side = swap_heads(side_out)
    arrived = route(packed)
    gate, queries, vk = call(
        unpack_kernel, [head_part, head_part, shape(PART, 2 * HEAD_DIM)],
        (ids, *side, arrived), (1,) + (0,) * 5,
        flops=1 << 28, nbytes=2 << 20,
    )
    vk_parts = (from_quarter(vk, -1), from_quarter(vk, -2), vk)
    query_parts = (from_quarter(queries, 2), from_quarter(queries, 1))
    held = pltpu.VMEM((PART, 2 * HEAD_DIM), BF16)
    done = pltpu.VMEM((2, PART, HEAD_DIM), BF16)
    mixed, gate_grad, *layer = call(
        forward_kernel, [head_part, head_part, *pieces],
        (ids, lengths, *side, gate, queries, *vk_parts), (1, 1) + (0,) * 9,
        scratch=[held], flops=1 << 29, nbytes=2 << 20,
    )
    mixed_parts = (from_quarter(mixed, 2), from_quarter(mixed, 1))
    layer_home = swap_heads(layer)
    gq_back, own, picks = call(
        query_grad_kernel,
        [half_chunked, shape(2, PART, HEAD_DIM, dtype=F32), shape(HEADS, N_DP * CHUNK, 2 * ROWS)],
        (ids, lengths, *side, mixed, gate_grad, queries, *vk_parts), (1, 1) + (0,) * 10,
        scratch=[done], flops=1 << 29, nbytes=2 << 20,
    )
    (back,) = call(
        backward_kernel, [chunked],
        (ids, lengths, picks, vk, *query_parts, *mixed_parts, own, gq_back),
        (1, 1) + (0,) * 8,
        scratch=[done, pltpu.VMEM(chunked.shape, BF16), pltpu.SemaphoreType.DMA((HEADS,))],
        flops=1 << 30, nbytes=3 << 20, hbm_out=True,
    )
    returned = route(back)
    grad_projected, layer_output = call(
        finish_kernel, [shape(ROWS, 4 * HEADS * HEAD_DIM), shape(ROWS, HEADS * HEAD_DIM)],
        (ids, home, *layer_home, returned), (1, 0, 0, 0, 0, 0, 0),
        scratch=[
            pltpu.VMEM(projected.shape, BF16), pltpu.VMEM(grad_out.shape, BF16),
            pltpu.SemaphoreType.DMA((5 * HEADS + 1,)),
        ],
        flops=1 << 28, nbytes=2 << 20, hbm_out=True,
    )
    return (layer_output, grad_projected)


def solution(mesh):
    fine = Mesh(mesh.devices.reshape(N_DP, N_X, HEADS), ("dp", "x", "h"))
    rows = P(("dp", "x", "h"), None)
    in_specs = (rows, P(("x", "h"), None), P("dp", None), rows)
    return jax.shard_map(
        body, mesh=fine, in_specs=in_specs, out_specs=(rows, rows), check_vma=False
    )
```

```python
import functools

import jax
import jax.numpy as jnp
from jax import lax
from jax.experimental import pallas as pl
from jax.experimental.pallas import tpu as pltpu
from jax.sharding import Mesh
from jax.sharding import PartitionSpec as P

HEADS = 4
HEAD_DIM = 128
BLOCK = 128
USERS = 3
EPSILON = 1e-06
SCALE = HEAD_DIM ** (-0.5)
ROWS = 128
CAP = 8
N_DP = 32
N_X = 4
REACH = 2
PART = HEADS * ROWS
GROUP = N_X * PART
STEP = 256
VMEM_LIMIT = 48 * 1024 * 1024
CHUNK = 2 * CAP

F32 = jnp.float32
BF16 = jnp.bfloat16


def dot_nn(a, b):
    return lax.dot_general(a, b, (((1,), (0,)), ((), ())), preferred_element_type=F32)


def dot_nt(a, b):
    return lax.dot_general(a, b, (((1,), (1,)), ((), ())), preferred_element_type=F32)


def iota(shape, dim):
    return lax.broadcasted_iota(jnp.int32, shape, dim)


def call(kernel, outs, ins, smem=(), scratch=(), flops=0, nbytes=0, hbm_in=(), hbm_out=False, limit=VMEM_LIMIT):
    spaces = [pltpu.VMEM] * len(ins)
    for n in smem:
        spaces[n] = pltpu.SMEM
    for n in hbm_in:
        spaces[n] = pl.ANY
    return pl.pallas_call(
        kernel,
        out_shape=outs,
        in_specs=[pl.BlockSpec(memory_space=space) for space in spaces],
        out_specs=[pl.BlockSpec(memory_space=pl.ANY if hbm_out else pltpu.VMEM)] * len(outs),
        scratch_shapes=list(scratch),
        compiler_params=pltpu.CompilerParams(vmem_limit_bytes=limit),
        name=kernel.__name__,
        cost_estimate=pl.CostEstimate(flops=flops, bytes_accessed=nbytes, transcendentals=0),
    )(*ins)


def shape(*dims, dtype=BF16):
    return jax.ShapeDtypeStruct(dims, dtype)


def owners_of(dest_ref, dp):
    targets = dest_ref[pl.ds(dp, 1), :]
    owners = lax.shift_right_logical(targets, 7).astype(F32)
    across = jnp.broadcast_to(owners, (ROWS, ROWS))
    return across, across.T


def pack_kernel(dest_ref, proj_ref, out_ref, proj, packed, in_sem, out_sems):
    load = pltpu.make_async_copy(proj_ref, proj, in_sem)
    load.start()
    across, down = owners_of(dest_ref, lax.axis_index("dp"))
    square = (ROWS, ROWS)
    earlier = (across == down) & (iota(square, 0) < iota(square, 1))
    slot = jnp.sum(jnp.where(earlier, 1.0, 0.0), axis=0, keepdims=True)
    key = (across[0:1] * CAP + slot).astype(jnp.int32)
    pick = jnp.where(iota((N_DP * CAP, ROWS), 0) == key, 1.0, 0.0).astype(BF16)
    load.wait()
    stores = []
    for pair in range(0, HEADS, 2):
        for j in range(2):
            halves = []
            for block in (j, 2 + j):
                at = (block * HEADS + pair) * HEAD_DIM
                moved = dot_nn(pick, proj[:, at : at + 2 * HEAD_DIM])
                halves.append(moved.reshape(N_DP, CAP, 2 * HEAD_DIM))
            chunks = jnp.concatenate(halves, axis=1).astype(BF16)
            for h in range(2):
                packed[:, pair + h, :, j * HEAD_DIM : (j + 1) * HEAD_DIM] = chunks[
                    :, :, h * HEAD_DIM : (h + 1) * HEAD_DIM
                ]
        heads = slice(pair, pair + 2)
        stores.append(
            pltpu.make_async_copy(packed.at[:, heads], out_ref.at[:, heads], out_sems.at[pair // 2])
        )
        stores[-1].start()
    for store in stores:
        store.wait()


def head_columns(h):
    return pl.ds(pl.multiple_of(h * HEAD_DIM, HEAD_DIM), HEAD_DIM)


def block_rows(c):
    return pl.ds(pl.multiple_of(c * ROWS, ROWS), ROWS)


def user_bounds(lengths_ref):
    bounds, start = [], jnp.int32(0)
    for u in range(USERS):
        length = lengths_ref[0, u]
        padded = (length + BLOCK - 1) // BLOCK * BLOCK
        bounds.append((start, start + length, start + padded))
        start = start + padded
    return bounds


def first_key(positions, bounds):
    low = jnp.full(positions.shape, 2 * GROUP, jnp.int32)
    for start, end, _ in bounds:
        low = jnp.where((positions >= start) & (positions < end), start, low)
    return low


def side_kernel(lengths_ref, dest_ref, grad_ref, *out_refs):
    *out_refs, home_ref, low_ref, low_rows_ref = out_refs
    bounds = user_bounds(lengths_ref)
    base = lax.axis_index("x") * PART
    low_ref[...] = first_key(base + iota(low_ref.shape, 0), bounds)
    low_rows_ref[...] = first_key(base + iota(low_rows_ref.shape, 1), bounds)
    across, down = owners_of(dest_ref, lax.axis_index("dp"))
    earlier = (across == down) & (iota((ROWS, ROWS), 1) < iota((ROWS, ROWS), 0))
    rank = jnp.sum(jnp.where(earlier, 1.0, 0.0), axis=1, keepdims=True)
    home_ref[...] = pick_down((down[:, 0:1] * CAP + rank).astype(jnp.int32))
    group = lax.axis_index("dp")
    mapping = dest_ref[...]
    landing = lax.shift_right_logical(mapping, 7) == group
    landing_f = jnp.where(landing, 1.0, 0.0)
    square = (ROWS, ROWS)
    before = jnp.where(iota(square, 0) < iota(square, 1), 1.0, 0.0).astype(BF16)
    slot = dot_nn(landing_f.astype(BF16), before)
    code = iota((N_DP, ROWS), 0).astype(F32) * CAP + slot
    place = jnp.where(landing, mapping & (ROWS - 1), ROWS)
    row_of = iota(square, 0)
    total = jnp.zeros(square, F32)
    for i in range(N_DP):
        total = total + jnp.where(row_of == place[i : i + 1], code[i : i + 1], 0.0)
    codes = jnp.broadcast_to(jnp.sum(total, axis=1, keepdims=True), square).T
    for k, out_ref in enumerate(out_refs):
        out_ref[:ROWS] = grad_ref[:, head_columns(lax.axis_index("h") ^ k)]
        out_ref[ROWS:] = codes[:CHUNK].astype(BF16)


def chunk_row(code, half):
    return (code >> 3) * CHUNK + half * CAP + (code & (CAP - 1))


def code_across(side_ref):
    return side_ref[ROWS : ROWS + CHUNK].astype(F32)[0:1]


def both_halves(code, axis):
    return jnp.concatenate([chunk_row(code, half) for half in range(2)], axis=axis)


def pick_down(code):
    lane = iota((2 * ROWS, N_DP * CHUNK), 1)
    return jnp.where(lane == both_halves(code, 0), 1.0, 0.0).astype(BF16)


def code_of_block(c, head, sides):
    code = jnp.zeros((1, ROWS), F32)
    for k, side_ref in enumerate(sides):
        code = jnp.where((head ^ k) == c, code_across(side_ref), code)
    return code


def unpack_kernel(
    s0, s1, s2, s3, arrived_ref, gate_ref, query_ref, vk_ref,
):
    for c in range(HEADS):
        rows = slice(c * ROWS, (c + 1) * ROWS)
        code = code_of_block(c, lax.axis_index("h"), (s0, s1, s2, s3))
        code = jnp.broadcast_to(code, (ROWS, ROWS)).T.astype(jnp.int32)
        chunks = arrived_ref[:, c].reshape(N_DP * CHUNK, 2 * HEAD_DIM)
        moved = dot_nn(pick_down(code[:, 0:1]), chunks).astype(BF16)
        gate_ref[rows] = moved[:ROWS, :HEAD_DIM]
        vk_ref[rows, :HEAD_DIM] = moved[:ROWS, HEAD_DIM:]
        query_ref[rows] = moved[ROWS:, :HEAD_DIM]
        vk_ref[rows, HEAD_DIM:] = moved[ROWS:, HEAD_DIM:]


def half_scores(a, b):
    return dot_nt(a, b) * (0.5 * SCALE)


def silu_of(half, tanh):
    return half + half * tanh


def slope_of(half, tanh):
    return (0.5 + 0.5 * tanh) * (1.0 + half * (1.0 - tanh))


def low_down(low_ref):
    return jnp.concatenate([low_ref[...]] * (STEP // ROWS), axis=1)


def pairs_allowed(key_pos, query_pos, low):
    return (key_pos >= low) & (key_pos <= query_pos)


def steps_of(parts, quarters):
    for part, quarter in zip(parts, quarters):
        for at in range(0, PART, STEP):
            yield part, slice(at, at + STEP), quarter * PART + at


def forward_kernel(
    low_ref, s0, s1, s2, s3, gate_ref, query_ref, vk1_ref, vk2_ref, vk0_ref,
    mixed_ref, gate_grad_ref, l0, l1, l2, l3, held,
):
    low = low_down(low_ref)
    quarter = lax.axis_index("x")
    query_pos = quarter * PART + iota((PART, 1), 0)
    queries = query_ref[...]
    mixed_sum = jnp.zeros((PART, HEAD_DIM), F32)
    for vk_ref, rows, at in steps_of(
        (vk2_ref, vk1_ref, vk0_ref), (quarter - 2, quarter - 1, quarter)
    ):
        half = half_scores(queries, vk_ref[rows, HEAD_DIM:])
        allowed = pairs_allowed(at + iota((1, STEP), 1), query_pos, low)
        weights = jnp.where(allowed, silu_of(half, jnp.tanh(half)), 0.0).astype(BF16)
        mixed_sum = mixed_sum + dot_nn(weights, vk_ref[rows, :HEAD_DIM])
    center = mixed_sum - jnp.mean(mixed_sum, axis=-1, keepdims=True)
    inverse = lax.rsqrt(jnp.mean(center * center, axis=-1, keepdims=True) + EPSILON)
    normed = center * inverse
    gating = gate_ref[...].astype(F32)
    head = lax.axis_index("h")
    for k, part in enumerate((s0, s1, s2, s3)):
        held[block_rows(head ^ k), HEAD_DIM:] = part[:ROWS]
    upstream = held[:, HEAD_DIM:].astype(F32)
    layer = (normed * gating).astype(BF16)
    grad_normed = upstream * gating
    mixed_ref[...] = (
        (
            grad_normed
            - jnp.mean(grad_normed, axis=-1, keepdims=True)
            - normed * jnp.mean(grad_normed * normed, axis=-1, keepdims=True)
        )
        * inverse
    ).astype(BF16)
    gate_grad_ref[...] = (upstream * normed).astype(BF16)
    held[:, :HEAD_DIM] = layer
    for k, layer_ref in enumerate((l0, l1, l2, l3)):
        layer_ref[...] = held[block_rows(head ^ k), :HEAD_DIM]


def key_grads(keys, values, key_pos, queries, grad_mixed, query_pos, low):
    half = half_scores(keys, queries)
    allowed = pairs_allowed(key_pos, query_pos, low)
    tanh = jnp.tanh(half)
    weights = jnp.where(allowed, silu_of(half, tanh), 0.0).astype(BF16)
    slope = jnp.where(allowed, slope_of(half, tanh), 0.0)
    grad_scores = (dot_nt(values, grad_mixed) * slope).astype(BF16)
    return dot_nn(weights, grad_mixed), dot_nn(grad_scores, queries)


def query_grad_kernel(
    low_ref, low_rows_ref, s0, s1, s2, s3, mixed_ref, gate_grad_ref, query_ref,
    vk1_ref, vk2_ref, vk0_ref, out_ref, own_ref, picks_ref, done,
):
    low = low_down(low_ref)
    quarter = lax.axis_index("x")
    own_pos = quarter * PART + iota((PART, 1), 0)
    queries = query_ref[...]
    grad_mixed = mixed_ref[...]
    total = jnp.zeros((PART, HEAD_DIM), F32)
    for vk_ref, rows, at in steps_of(
        (vk2_ref, vk1_ref, vk0_ref), (quarter - 2, quarter - 1, quarter)
    ):
        keys = vk_ref[rows, HEAD_DIM:]
        half = half_scores(queries, keys)
        allowed = pairs_allowed(at + iota((1, STEP), 1), own_pos, low)
        slope = jnp.where(allowed, slope_of(half, jnp.tanh(half)), 0.0)
        grad_scores = (dot_nt(grad_mixed, vk_ref[rows, :HEAD_DIM]) * slope).astype(BF16)
        total = total + dot_nn(grad_scores, keys)
    done[0] = gate_grad_ref[...]
    done[1] = (total * SCALE).astype(BF16)
    back_picks((s0, s1, s2, s3), picks_ref)
    pack_back(picks_ref, done, out_ref, 0)
    values, keys = vk0_ref[:, :HEAD_DIM], vk0_ref[:, HEAD_DIM:]
    sums = (0.0, 0.0)
    for part, rows, at in steps_of((query_ref,), (quarter,)):
        terms = key_grads(
            keys, values, own_pos, part[rows], mixed_ref[rows], at + iota((1, STEP), 1),
            low_rows_ref[0:1, rows],
        )
        sums = tuple(a + b for a, b in zip(sums, terms))
    for n in range(2):
        own_ref[n] = sums[n]


def back_picks(sides, picks_ref):
    sublane = iota((N_DP * CHUNK, 2 * ROWS), 0)
    for k, side_ref in enumerate(sides):
        at = both_halves(code_across(side_ref).astype(jnp.int32), 1)
        picks_ref[lax.axis_index("h") ^ k] = jnp.where(sublane == at, 1.0, 0.0).astype(BF16)


def pack_back(picks_ref, done, out_ref, j, finished=lambda c: None):
    for c in range(HEADS):
        rows = slice(c * ROWS, (c + 1) * ROWS)
        both = jnp.concatenate([done[0, rows], done[1, rows]], axis=0)
        out_ref[:, c, :, j * HEAD_DIM : (j + 1) * HEAD_DIM] = (
            dot_nn(picks_ref[c], both).astype(BF16).reshape(N_DP, CHUNK, HEAD_DIM)
        )
        finished(c)


def backward_kernel(
    low_rows_ref, picks_ref, vk_ref, q2_ref, q1_ref, m2_ref, m1_ref,
    own_ref, gq_ref, out_ref, done, packed, sems,
):
    packed[:, :, :, :HEAD_DIM] = gq_ref[...]
    quarter = lax.axis_index("x")
    own_pos = quarter * PART + iota((PART, 1), 0)
    values, keys = vk_ref[:, :HEAD_DIM], vk_ref[:, HEAD_DIM:]
    sums = (own_ref[0], own_ref[1])
    later = steps_of(((q1_ref, m1_ref), (q2_ref, m2_ref)), (quarter + 1, quarter + 2))
    for n, ((part, mixed), rows, at) in enumerate(later):
        along = PART + n * STEP
        terms = key_grads(
            keys, values, own_pos, part[rows], mixed[rows], at + iota((1, STEP), 1),
            low_rows_ref[0:1, along : along + STEP],
        )
        sums = tuple(a + b for a, b in zip(sums, terms))
    done[0] = sums[0].astype(BF16)
    done[1] = (sums[1] * SCALE).astype(BF16)
    stores = []

    def send(c):
        stores.append(pltpu.make_async_copy(packed.at[:, c], out_ref.at[:, c], sems.at[c]))
        stores[-1].start()

    pack_back(picks_ref, done, packed, 1, send)
    for store in stores:
        store.wait()


def finish_kernel(
    home_ref, l0, l1, l2, l3, back_ref, grad_ref, out_ref, grads, sems
):
    stores = []
    for k, layer_ref in enumerate((l0, l1, l2, l3)):
        columns = head_columns(lax.axis_index("h") ^ k)
        stores.append(pltpu.make_async_copy(layer_ref, out_ref.at[:, columns], sems.at[k]))
        stores[-1].start()
    pick = home_ref[...]
    for h in range(HEADS):
        chunks = back_ref[:, h].reshape(N_DP * CHUNK, 2 * HEAD_DIM)
        moved = dot_nn(pick, chunks).astype(BF16)
        for half in range(2):
            for j in range(2):
                block = 2 * half + j
                at = (block * HEADS + h) * HEAD_DIM
                columns = slice(at, at + HEAD_DIM)
                grads[:, columns] = moved[
                    half * ROWS : (half + 1) * ROWS, j * HEAD_DIM : (j + 1) * HEAD_DIM
                ]
                stores.append(
                    pltpu.make_async_copy(
                        grads.at[:, columns], grad_ref.at[:, columns], sems.at[HEADS + 4 * h + block]
                    )
                )
                stores[-1].start()
    for store in stores:
        store.wait()


def route(chunks):
    flat = chunks.reshape(N_DP * HEADS * CHUNK, 2 * HEAD_DIM)
    moved = lax.all_to_all(flat, ("dp", "h"), 0, 0, tiled=True)
    return moved.reshape(chunks.shape)


def from_quarter(array, by):
    pairs = [(i, i - by) for i in range(N_X) if 0 <= i - by < N_X]
    return lax.ppermute(array, "x", pairs)


def swap_heads(pieces):
    moved = [
        lax.ppermute(piece, "h", [(i, i ^ k) for i in range(HEADS)])
        for k, piece in enumerate(pieces)
        if k
    ]
    return [pieces[0], *moved]


def body(projected, destination, lengths, grad_out):
    mapping = destination.reshape(N_DP, ROWS)
    chunked = shape(N_DP, HEADS, CHUNK, 2 * HEAD_DIM)
    half_chunked = shape(N_DP, HEADS, CHUNK, HEAD_DIM)
    head_part = shape(PART, HEAD_DIM)
    pieces = [shape(ROWS, HEAD_DIM)] * HEADS
    dma = pltpu.SemaphoreType.DMA
    (packed,) = call(
        pack_kernel, [chunked], (mapping, projected),
        scratch=[
            pltpu.VMEM(projected.shape, BF16), pltpu.VMEM(chunked.shape, BF16), dma, dma((2,)),
        ],
        flops=2 * 256 * 128 * 2048, nbytes=3 << 19,
        hbm_in=(1,), hbm_out=True, limit=62 * 1024 * 1024,
    )
    *side_out, home, low, low_rows = call(
        side_kernel,
        [shape(ROWS + CHUNK, HEAD_DIM)] * HEADS
        + [
            shape(2 * ROWS, N_DP * CHUNK), shape(PART, ROWS, dtype=jnp.int32),
            shape(8, (REACH + 1) * PART, dtype=jnp.int32),
        ],
        (lengths, mapping, grad_out), smem=(0,), nbytes=3 << 17,
    )
    side = swap_heads(side_out)
    arrived = route(packed)
    gate, queries, vk = call(
        unpack_kernel, [head_part, head_part, shape(PART, 2 * HEAD_DIM)], (*side, arrived),
        flops=1 << 28, nbytes=2 << 20,
    )
    vk_parts = (from_quarter(vk, -1), from_quarter(vk, -2), vk)
    query_parts = (from_quarter(queries, 2), from_quarter(queries, 1))
    held = pltpu.VMEM((PART, 2 * HEAD_DIM), BF16)
    done = pltpu.VMEM((2, PART, HEAD_DIM), BF16)
    mixed, gate_grad, *layer = call(
        forward_kernel, [head_part, head_part, *pieces],
        (low, *side, gate, queries, *vk_parts),
        scratch=[held], flops=1 << 29, nbytes=2 << 20,
    )
    mixed_parts = (from_quarter(mixed, 2), from_quarter(mixed, 1))
    layer_home = swap_heads(layer)
    gq_back, own, picks = call(
        query_grad_kernel,
        [half_chunked, shape(2, PART, HEAD_DIM, dtype=F32), shape(HEADS, N_DP * CHUNK, 2 * ROWS)],
        (low, low_rows, *side, mixed, gate_grad, queries, *vk_parts),
        scratch=[done], flops=1 << 29, nbytes=2 << 20,
    )
    (back,) = call(
        backward_kernel, [chunked],
        (low_rows, picks, vk, *query_parts, *mixed_parts, own, gq_back),
        scratch=[done, pltpu.VMEM(chunked.shape, BF16), dma((HEADS,))],
        flops=1 << 30, nbytes=3 << 20, hbm_out=True,
    )
    returned = route(back)
    grad_projected, layer_output = call(
        finish_kernel, [shape(ROWS, 4 * HEADS * HEAD_DIM), shape(ROWS, HEADS * HEAD_DIM)],
        (home, *layer_home, returned),
        scratch=[pltpu.VMEM(projected.shape, BF16), dma((5 * HEADS,))],
        flops=1 << 28, nbytes=2 << 20, hbm_out=True,
    )
    return (layer_output, grad_projected)


def solution(mesh):
    fine = Mesh(mesh.devices.reshape(N_DP, N_X, HEADS), ("dp", "x", "h"))
    rows = P(("dp", "x", "h"), None)
    in_specs = (rows, P(("x", "h"), None), P("dp", None), rows)
    return jax.shard_map(
        body, mesh=fine, in_specs=in_specs, out_specs=(rows, rows), check_vma=False
    )
```

```python
import functools

import jax
import jax.numpy as jnp
from jax import lax
from jax.experimental import pallas as pl
from jax.experimental.pallas import tpu as pltpu
from jax.sharding import Mesh
from jax.sharding import PartitionSpec as P

HEADS = 4
HEAD_DIM = 128
BLOCK = 128
USERS = 3
EPSILON = 1e-06
SCALE = HEAD_DIM ** (-0.5)
ROWS = 128
CAP = 8
N_DP = 32
N_X = 4
REACH = 2
PART = HEADS * ROWS
GROUP = N_X * PART
STEP = 256
VMEM_LIMIT = 48 * 1024 * 1024
CHUNK = 2 * CAP

F32 = jnp.float32
BF16 = jnp.bfloat16


def dot_nn(a, b):
    return lax.dot_general(a, b, (((1,), (0,)), ((), ())), preferred_element_type=F32)


def dot_nt(a, b):
    return lax.dot_general(a, b, (((1,), (1,)), ((), ())), preferred_element_type=F32)


def iota(shape, dim):
    return lax.broadcasted_iota(jnp.int32, shape, dim)


def call(kernel, outs, ins, smem=(), scratch=(), flops=0, nbytes=0, hbm_in=(), hbm_out=False, limit=VMEM_LIMIT):
    spaces = [pltpu.VMEM] * len(ins)
    for n in smem:
        spaces[n] = pltpu.SMEM
    for n in hbm_in:
        spaces[n] = pl.ANY
    return pl.pallas_call(
        kernel,
        out_shape=outs,
        in_specs=[pl.BlockSpec(memory_space=space) for space in spaces],
        out_specs=[pl.BlockSpec(memory_space=pl.ANY if hbm_out else pltpu.VMEM)] * len(outs),
        scratch_shapes=list(scratch),
        compiler_params=pltpu.CompilerParams(vmem_limit_bytes=limit),
        name=kernel.__name__,
        cost_estimate=pl.CostEstimate(flops=flops, bytes_accessed=nbytes, transcendentals=0),
    )(*ins)


def shape(*dims, dtype=BF16):
    return jax.ShapeDtypeStruct(dims, dtype)


def owners_of(dest_ref, dp):
    targets = dest_ref[pl.ds(dp, 1), :]
    owners = lax.shift_right_logical(targets, 7).astype(F32)
    across = jnp.broadcast_to(owners, (ROWS, ROWS))
    return across, across.T


def pack_kernel(dest_ref, proj_ref, out_ref, proj, packed, in_sem, out_sems):
    load = pltpu.make_async_copy(proj_ref, proj, in_sem)
    load.start()
    across, down = owners_of(dest_ref, lax.axis_index("dp"))
    square = (ROWS, ROWS)
    earlier = (across == down) & (iota(square, 0) < iota(square, 1))
    slot = jnp.sum(jnp.where(earlier, 1.0, 0.0), axis=0, keepdims=True)
    key = (across[0:1] * CAP + slot).astype(jnp.int32)
    pick = jnp.where(iota((N_DP * CAP, ROWS), 0) == key, 1.0, 0.0).astype(BF16)
    load.wait()
    stores = []
    for pair in range(0, HEADS, 2):
        for j in range(2):
            halves = []
            for block in (j, 2 + j):
                at = (block * HEADS + pair) * HEAD_DIM
                moved = dot_nn(pick, proj[:, at : at + 2 * HEAD_DIM])
                halves.append(moved.reshape(N_DP, CAP, 2 * HEAD_DIM))
            chunks = jnp.concatenate(halves, axis=1).astype(BF16)
            for h in range(2):
                packed[:, pair + h, :, j * HEAD_DIM : (j + 1) * HEAD_DIM] = chunks[
                    :, :, h * HEAD_DIM : (h + 1) * HEAD_DIM
                ]
        heads = slice(pair, pair + 2)
        stores.append(
            pltpu.make_async_copy(packed.at[:, heads], out_ref.at[:, heads], out_sems.at[pair // 2])
        )
        stores[-1].start()
    for store in stores:
        store.wait()


def head_columns(h):
    return pl.ds(pl.multiple_of(h * HEAD_DIM, HEAD_DIM), HEAD_DIM)


def block_rows(c):
    return pl.ds(pl.multiple_of(c * ROWS, ROWS), ROWS)


def user_bounds(lengths_ref):
    bounds, start = [], jnp.int32(0)
    for u in range(USERS):
        length = lengths_ref[0, u]
        padded = (length + BLOCK - 1) // BLOCK * BLOCK
        bounds.append((start, start + length, start + padded))
        start = start + padded
    return bounds


def first_key(positions, bounds):
    low = jnp.full(positions.shape, 2 * GROUP, jnp.int32)
    for start, end, _ in bounds:
        low = jnp.where((positions >= start) & (positions < end), start, low)
    return low


def side_kernel(lengths_ref, dest_ref, grad_ref, *out_refs):
    *out_refs, home_ref, low_ref, low_rows_ref = out_refs
    bounds = user_bounds(lengths_ref)
    base = lax.axis_index("x") * PART
    low_ref[...] = first_key(base + iota(low_ref.shape, 0), bounds)
    low_rows_ref[...] = first_key(base + iota(low_rows_ref.shape, 1), bounds)
    across, down = owners_of(dest_ref, lax.axis_index("dp"))
    earlier = (across == down) & (iota((ROWS, ROWS), 1) < iota((ROWS, ROWS), 0))
    rank = jnp.sum(jnp.where(earlier, 1.0, 0.0), axis=1, keepdims=True)
    home_ref[...] = pick_down((down[:, 0:1] * CAP + rank).astype(jnp.int32))
    group = lax.axis_index("dp")
    mapping = dest_ref[...]
    landing = lax.shift_right_logical(mapping, 7) == group
    landing_f = jnp.where(landing, 1.0, 0.0)
    square = (ROWS, ROWS)
    before = jnp.where(iota(square, 0) < iota(square, 1), 1.0, 0.0).astype(BF16)
    slot = dot_nn(landing_f.astype(BF16), before)
    code = iota((N_DP, ROWS), 0).astype(F32) * CAP + slot
    place = jnp.where(landing, mapping & (ROWS - 1), ROWS)
    row_of = iota(square, 0)
    total = jnp.zeros(square, F32)
    for i in range(N_DP):
        total = total + jnp.where(row_of == place[i : i + 1], code[i : i + 1], 0.0)
    codes = jnp.broadcast_to(jnp.sum(total, axis=1, keepdims=True), square).T
    for k, out_ref in enumerate(out_refs):
        out_ref[:ROWS] = grad_ref[:, head_columns(lax.axis_index("h") ^ k)]
        out_ref[ROWS:] = codes[:CHUNK].astype(BF16)


def chunk_row(code, half):
    return (code >> 3) * CHUNK + half * CAP + (code & (CAP - 1))


def code_across(side_ref):
    return side_ref[ROWS : ROWS + CHUNK].astype(F32)[0:1]


def both_halves(code, axis):
    return jnp.concatenate([chunk_row(code, half) for half in range(2)], axis=axis)


def pick_down(code):
    lane = iota((2 * ROWS, N_DP * CHUNK), 1)
    return jnp.where(lane == both_halves(code, 0), 1.0, 0.0).astype(BF16)


def code_of_block(c, head, sides):
    code = jnp.zeros((1, ROWS), F32)
    for k, side_ref in enumerate(sides):
        code = jnp.where((head ^ k) == c, code_across(side_ref), code)
    return code


def unpack_kernel(
    s0, s2, s3, s1, arrived_ref, gate_ref, query_ref, vk_ref,
):
    for c in range(HEADS):
        rows = slice(c * ROWS, (c + 1) * ROWS)
        code = code_of_block(c, lax.axis_index("h"), (s0, s1, s2, s3))
        code = jnp.broadcast_to(code, (ROWS, ROWS)).T.astype(jnp.int32)
        chunks = arrived_ref[:, c].reshape(N_DP * CHUNK, 2 * HEAD_DIM)
        moved = dot_nn(pick_down(code[:, 0:1]), chunks).astype(BF16)
        gate_ref[rows] = moved[:ROWS, :HEAD_DIM]
        vk_ref[rows, :HEAD_DIM] = moved[:ROWS, HEAD_DIM:]
        query_ref[rows] = moved[ROWS:, :HEAD_DIM]
        vk_ref[rows, HEAD_DIM:] = moved[ROWS:, HEAD_DIM:]


def half_scores(a, b):
    return dot_nt(a, b) * (0.5 * SCALE)


def silu_of(half, tanh):
    return half + half * tanh


def slope_of(half, tanh):
    return (0.5 + 0.5 * tanh) * (1.0 + half * (1.0 - tanh))


def low_down(low_ref):
    return jnp.concatenate([low_ref[...]] * (STEP // ROWS), axis=1)


def pairs_allowed(key_pos, query_pos, low):
    return (key_pos >= low) & (key_pos <= query_pos)


def steps_of(parts, quarters):
    for part, quarter in zip(parts, quarters):
        for at in range(0, PART, STEP):
            yield part, slice(at, at + STEP), quarter * PART + at


def forward_kernel(
    low_ref, s0, s2, s3, s1, gate_ref, query_ref, vk1_ref, vk2_ref, vk0_ref,
    mixed_ref, gate_grad_ref, l0, l1, l2, l3, held,
):
    low = low_down(low_ref)
    quarter = lax.axis_index("x")
    query_pos = quarter * PART + iota((PART, 1), 0)
    queries = query_ref[...]
    mixed_sum = jnp.zeros((PART, HEAD_DIM), F32)
    for vk_ref, rows, at in steps_of(
        (vk2_ref, vk1_ref, vk0_ref), (quarter - 2, quarter - 1, quarter)
    ):
        half = half_scores(queries, vk_ref[rows, HEAD_DIM:])
        allowed = pairs_allowed(at + iota((1, STEP), 1), query_pos, low)
        weights = jnp.where(allowed, silu_of(half, jnp.tanh(half)), 0.0).astype(BF16)
        mixed_sum = mixed_sum + dot_nn(weights, vk_ref[rows, :HEAD_DIM])
    center = mixed_sum - jnp.mean(mixed_sum, axis=-1, keepdims=True)
    inverse = lax.rsqrt(jnp.mean(center * center, axis=-1, keepdims=True) + EPSILON)
    normed = center * inverse
    gating = gate_ref[...].astype(F32)
    head = lax.axis_index("h")
    for k, part in enumerate((s0, s1, s2, s3)):
        held[block_rows(head ^ k), HEAD_DIM:] = part[:ROWS]
    upstream = held[:, HEAD_DIM:].astype(F32)
    layer = (normed * gating).astype(BF16)
    grad_normed = upstream * gating
    mixed_ref[...] = (
        (
            grad_normed
            - jnp.mean(grad_normed, axis=-1, keepdims=True)
            - normed * jnp.mean(grad_normed * normed, axis=-1, keepdims=True)
        )
        * inverse
    ).astype(BF16)
    gate_grad_ref[...] = (upstream * normed).astype(BF16)
    held[:, :HEAD_DIM] = layer
    for k, layer_ref in enumerate((l0, l1, l2, l3)):
        layer_ref[...] = held[block_rows(head ^ k), :HEAD_DIM]


def key_grads(keys, values, key_pos, queries, grad_mixed, query_pos, low):
    half = half_scores(keys, queries)
    allowed = pairs_allowed(key_pos, query_pos, low)
    tanh = jnp.tanh(half)
    weights = jnp.where(allowed, silu_of(half, tanh), 0.0).astype(BF16)
    slope = jnp.where(allowed, slope_of(half, tanh), 0.0)
    grad_scores = (dot_nt(values, grad_mixed) * slope).astype(BF16)
    return dot_nn(weights, grad_mixed), dot_nn(grad_scores, queries)


def query_grad_kernel(
    low_ref, low_rows_ref, s0, s2, s3, s1, mixed_ref, gate_grad_ref, query_ref,
    vk1_ref, vk2_ref, vk0_ref, out_ref, own_ref, picks_ref, done,
):
    low = low_down(low_ref)
    quarter = lax.axis_index("x")
    own_pos = quarter * PART + iota((PART, 1), 0)
    queries = query_ref[...]
    grad_mixed = mixed_ref[...]
    total = jnp.zeros((PART, HEAD_DIM), F32)
    for vk_ref, rows, at in steps_of(
        (vk2_ref, vk1_ref, vk0_ref), (quarter - 2, quarter - 1, quarter)
    ):
        keys = vk_ref[rows, HEAD_DIM:]
        half = half_scores(queries, keys)
        allowed = pairs_allowed(at + iota((1, STEP), 1), own_pos, low)
        slope = jnp.where(allowed, slope_of(half, jnp.tanh(half)), 0.0)
        grad_scores = (dot_nt(grad_mixed, vk_ref[rows, :HEAD_DIM]) * slope).astype(BF16)
        total = total + dot_nn(grad_scores, keys)
    done[0] = gate_grad_ref[...]
    done[1] = (total * SCALE).astype(BF16)
    back_picks((s0, s1, s2, s3), picks_ref)
    pack_back(picks_ref, done, out_ref, 0)
    values, keys = vk0_ref[:, :HEAD_DIM], vk0_ref[:, HEAD_DIM:]
    sums = (0.0, 0.0)
    for part, rows, at in steps_of((query_ref,), (quarter,)):
        terms = key_grads(
            keys, values, own_pos, part[rows], mixed_ref[rows], at + iota((1, STEP), 1),
            low_rows_ref[0:1, rows],
        )
        sums = tuple(a + b for a, b in zip(sums, terms))
    for n in range(2):
        own_ref[n] = sums[n]


def back_picks(sides, picks_ref):
    sublane = iota((N_DP * CHUNK, 2 * ROWS), 0)
    for k, side_ref in enumerate(sides):
        at = both_halves(code_across(side_ref).astype(jnp.int32), 1)
        picks_ref[lax.axis_index("h") ^ k] = jnp.where(sublane == at, 1.0, 0.0).astype(BF16)


def pack_back(picks_ref, done, out_ref, j, finished=lambda c: None):
    for c in range(HEADS):
        rows = slice(c * ROWS, (c + 1) * ROWS)
        both = jnp.concatenate([done[0, rows], done[1, rows]], axis=0)
        out_ref[:, c, :, j * HEAD_DIM : (j + 1) * HEAD_DIM] = (
            dot_nn(picks_ref[c], both).astype(BF16).reshape(N_DP, CHUNK, HEAD_DIM)
        )
        finished(c)


def backward_kernel(
    low_rows_ref, picks_ref, vk_ref, q2_ref, q1_ref, m2_ref, m1_ref,
    own_ref, gq_ref, out_ref, done, packed, sems,
):
    packed[:, :, :, :HEAD_DIM] = gq_ref[...]
    quarter = lax.axis_index("x")
    own_pos = quarter * PART + iota((PART, 1), 0)
    values, keys = vk_ref[:, :HEAD_DIM], vk_ref[:, HEAD_DIM:]
    sums = (own_ref[0], own_ref[1])
    later = steps_of(((q1_ref, m1_ref), (q2_ref, m2_ref)), (quarter + 1, quarter + 2))
    for n, ((part, mixed), rows, at) in enumerate(later):
        along = PART + n * STEP
        terms = key_grads(
            keys, values, own_pos, part[rows], mixed[rows], at + iota((1, STEP), 1),
            low_rows_ref[0:1, along : along + STEP],
        )
        sums = tuple(a + b for a, b in zip(sums, terms))
    done[0] = sums[0].astype(BF16)
    done[1] = (sums[1] * SCALE).astype(BF16)
    stores = []

    def send(c):
        stores.append(pltpu.make_async_copy(packed.at[:, c], out_ref.at[:, c], sems.at[c]))
        stores[-1].start()

    pack_back(picks_ref, done, packed, 1, send)
    for store in stores:
        store.wait()


def finish_kernel(
    home_ref, l0, l2, l3, l1, back_ref, grad_ref, out_ref, grads, sems
):
    stores = []
    for k, layer_ref in enumerate((l0, l1, l2, l3)):
        columns = head_columns(lax.axis_index("h") ^ k)
        stores.append(pltpu.make_async_copy(layer_ref, out_ref.at[:, columns], sems.at[k]))
        stores[-1].start()
    pick = home_ref[...]
    for h in range(HEADS):
        chunks = back_ref[:, h].reshape(N_DP * CHUNK, 2 * HEAD_DIM)
        moved = dot_nn(pick, chunks).astype(BF16)
        for half in range(2):
            for j in range(2):
                block = 2 * half + j
                at = (block * HEADS + h) * HEAD_DIM
                columns = slice(at, at + HEAD_DIM)
                grads[:, columns] = moved[
                    half * ROWS : (half + 1) * ROWS, j * HEAD_DIM : (j + 1) * HEAD_DIM
                ]
                stores.append(
                    pltpu.make_async_copy(
                        grads.at[:, columns], grad_ref.at[:, columns], sems.at[HEADS + 4 * h + block]
                    )
                )
                stores[-1].start()
    for store in stores:
        store.wait()


def route(chunks):
    flat = chunks.reshape(N_DP * HEADS * CHUNK, 2 * HEAD_DIM)
    moved = lax.all_to_all(flat, ("dp", "h"), 0, 0, tiled=True)
    return moved.reshape(chunks.shape)


def from_quarter(array, by):
    pairs = [(i, i - by) for i in range(N_X) if 0 <= i - by < N_X]
    return lax.ppermute(array, "x", pairs)


def swap_heads(pieces):
    return [pieces[0]] + [
        lax.ppermute(pieces[k], "h", [(i, i ^ k) for i in range(HEADS)]) for k in (2, 3, 1)
    ]


def body(projected, destination, lengths, grad_out):
    mapping = destination.reshape(N_DP, ROWS)
    chunked = shape(N_DP, HEADS, CHUNK, 2 * HEAD_DIM)
    half_chunked = shape(N_DP, HEADS, CHUNK, HEAD_DIM)
    head_part = shape(PART, HEAD_DIM)
    pieces = [shape(ROWS, HEAD_DIM)] * HEADS
    dma = pltpu.SemaphoreType.DMA
    (packed,) = call(
        pack_kernel, [chunked], (mapping, projected),
        scratch=[
            pltpu.VMEM(projected.shape, BF16), pltpu.VMEM(chunked.shape, BF16), dma, dma((2,)),
        ],
        flops=2 * 256 * 128 * 2048, nbytes=3 << 19,
        hbm_in=(1,), hbm_out=True, limit=62 * 1024 * 1024,
    )
    *side_out, home, low, low_rows = call(
        side_kernel,
        [shape(ROWS + CHUNK, HEAD_DIM)] * HEADS
        + [
            shape(2 * ROWS, N_DP * CHUNK), shape(PART, ROWS, dtype=jnp.int32),
            shape(8, (REACH + 1) * PART, dtype=jnp.int32),
        ],
        (lengths, mapping, grad_out), smem=(0,), nbytes=3 << 17,
    )
    side = swap_heads(side_out)
    arrived = route(packed)
    gate, queries, vk = call(
        unpack_kernel, [head_part, head_part, shape(PART, 2 * HEAD_DIM)], (*side, arrived),
        flops=1 << 28, nbytes=2 << 20,
    )
    vk_parts = (from_quarter(vk, -1), from_quarter(vk, -2), vk)
    query_parts = (from_quarter(queries, 2), from_quarter(queries, 1))
    held = pltpu.VMEM((PART, 2 * HEAD_DIM), BF16)
    done = pltpu.VMEM((2, PART, HEAD_DIM), BF16)
    mixed, gate_grad, *layer = call(
        forward_kernel, [head_part, head_part, *pieces],
        (low, *side, gate, queries, *vk_parts),
        scratch=[held], flops=1 << 29, nbytes=2 << 20,
    )
    mixed_parts = (from_quarter(mixed, 2), from_quarter(mixed, 1))
    layer_home = swap_heads(layer)
    gq_back, own, picks = call(
        query_grad_kernel,
        [half_chunked, shape(2, PART, HEAD_DIM, dtype=F32), shape(HEADS, N_DP * CHUNK, 2 * ROWS)],
        (low, low_rows, *side, mixed, gate_grad, queries, *vk_parts),
        scratch=[done], flops=1 << 29, nbytes=2 << 20,
    )
    (back,) = call(
        backward_kernel, [chunked],
        (low_rows, picks, vk, *query_parts, *mixed_parts, own, gq_back),
        scratch=[done, pltpu.VMEM(chunked.shape, BF16), dma((HEADS,))],
        flops=1 << 30, nbytes=3 << 20, hbm_out=True,
    )
    returned = route(back)
    grad_projected, layer_output = call(
        finish_kernel, [shape(ROWS, 4 * HEADS * HEAD_DIM), shape(ROWS, HEADS * HEAD_DIM)],
        (home, *layer_home, returned),
        scratch=[pltpu.VMEM(projected.shape, BF16), dma((5 * HEADS,))],
        flops=1 << 28, nbytes=2 << 20, hbm_out=True,
    )
    return (layer_output, grad_projected)


def solution(mesh):
    fine = Mesh(mesh.devices.reshape(N_DP, N_X, HEADS), ("dp", "x", "h"))
    rows = P(("dp", "x", "h"), None)
    in_specs = (rows, P(("x", "h"), None), P("dp", None), rows)
    return jax.shard_map(
        body, mesh=fine, in_specs=in_specs, out_specs=(rows, rows), check_vma=False
    )
```

```python
import functools

import jax
import jax.numpy as jnp
from jax import lax
from jax.experimental import pallas as pl
from jax.experimental.pallas import tpu as pltpu
from jax.sharding import Mesh
from jax.sharding import PartitionSpec as P

HEADS = 4
HEAD_DIM = 128
BLOCK = 128
USERS = 3
EPSILON = 1e-06
SCALE = HEAD_DIM ** (-0.5)
ROWS = 128
CAP = 8
N_DP = 32
N_X = 4
REACH = 2
PART = HEADS * ROWS
GROUP = N_X * PART
STEP = 256
VMEM_LIMIT = 48 * 1024 * 1024
CHUNK = 2 * CAP

F32 = jnp.float32
BF16 = jnp.bfloat16


def dot_nn(a, b):
    return lax.dot_general(a, b, (((1,), (0,)), ((), ())), preferred_element_type=F32)


def dot_nt(a, b):
    return lax.dot_general(a, b, (((1,), (1,)), ((), ())), preferred_element_type=F32)


def iota(shape, dim):
    return lax.broadcasted_iota(jnp.int32, shape, dim)


def call(kernel, outs, ins, smem=(), scratch=(), flops=0, nbytes=0, hbm_in=(), hbm_out=False, limit=VMEM_LIMIT):
    spaces = [pltpu.VMEM] * len(ins)
    for n in smem:
        spaces[n] = pltpu.SMEM
    for n in hbm_in:
        spaces[n] = pl.ANY
    return pl.pallas_call(
        kernel,
        out_shape=outs,
        in_specs=[pl.BlockSpec(memory_space=space) for space in spaces],
        out_specs=[pl.BlockSpec(memory_space=pl.ANY if hbm_out else pltpu.VMEM)] * len(outs),
        scratch_shapes=list(scratch),
        compiler_params=pltpu.CompilerParams(vmem_limit_bytes=limit),
        name=kernel.__name__,
        cost_estimate=pl.CostEstimate(flops=flops, bytes_accessed=nbytes, transcendentals=0),
    )(*ins)


def shape(*dims, dtype=BF16):
    return jax.ShapeDtypeStruct(dims, dtype)


def owners_of(dest_ref, dp):
    targets = dest_ref[pl.ds(dp, 1), :]
    owners = lax.shift_right_logical(targets, 7).astype(F32)
    across = jnp.broadcast_to(owners, (ROWS, ROWS))
    return across, across.T


def pack_kernel(dest_ref, proj_ref, out_ref, proj, packed, in_sem, out_sems):
    load = pltpu.make_async_copy(proj_ref, proj, in_sem)
    load.start()
    across, down = owners_of(dest_ref, lax.axis_index("dp"))
    square = (ROWS, ROWS)
    earlier = (across == down) & (iota(square, 0) < iota(square, 1))
    slot = jnp.sum(jnp.where(earlier, 1.0, 0.0), axis=0, keepdims=True)
    key = (across[0:1] * CAP + slot).astype(jnp.int32)
    pick = jnp.where(iota((N_DP * CAP, ROWS), 0) == key, 1.0, 0.0).astype(BF16)
    load.wait()
    stores = []
    for pair in range(0, HEADS, 2):
        for j in range(2):
            halves = []
            for block in (j, 2 + j):
                at = (block * HEADS + pair) * HEAD_DIM
                moved = dot_nn(pick, proj[:, at : at + 2 * HEAD_DIM])
                halves.append(moved.reshape(N_DP, CAP, 2 * HEAD_DIM))
            chunks = jnp.concatenate(halves, axis=1).astype(BF16)
            for h in range(2):
                packed[:, pair + h, :, j * HEAD_DIM : (j + 1) * HEAD_DIM] = chunks[
                    :, :, h * HEAD_DIM : (h + 1) * HEAD_DIM
                ]
        heads = slice(pair, pair + 2)
        stores.append(
            pltpu.make_async_copy(packed.at[:, heads], out_ref.at[:, heads], out_sems.at[pair // 2])
        )
        stores[-1].start()
    for store in stores:
        store.wait()


def head_columns(h):
    return pl.ds(pl.multiple_of(h * HEAD_DIM, HEAD_DIM), HEAD_DIM)


def block_rows(c):
    return pl.ds(pl.multiple_of(c * ROWS, ROWS), ROWS)


def user_bounds(lengths_ref):
    bounds, start = [], jnp.int32(0)
    for u in range(USERS):
        length = lengths_ref[0, u]
        padded = (length + BLOCK - 1) // BLOCK * BLOCK
        bounds.append((start, start + length, start + padded))
        start = start + padded
    return bounds


def first_key(positions, bounds):
    low = jnp.full(positions.shape, 2 * GROUP, jnp.int32)
    for start, end, _ in bounds:
        low = jnp.where((positions >= start) & (positions < end), start, low)
    return low


def side_kernel(lengths_ref, dest_ref, grad_ref, *out_refs):
    *out_refs, home_ref, low_ref, low_rows_ref = out_refs
    bounds = user_bounds(lengths_ref)
    base = lax.axis_index("x") * PART
    low_ref[...] = first_key(base + iota(low_ref.shape, 0), bounds)
    low_rows_ref[...] = first_key(base + iota(low_rows_ref.shape, 1), bounds)
    across, down = owners_of(dest_ref, lax.axis_index("dp"))
    earlier = (across == down) & (iota((ROWS, ROWS), 1) < iota((ROWS, ROWS), 0))
    rank = jnp.sum(jnp.where(earlier, 1.0, 0.0), axis=1, keepdims=True)
    home_ref[...] = pick_down((down[:, 0:1] * CAP + rank).astype(jnp.int32))
    group = lax.axis_index("dp")
    mapping = dest_ref[...]
    landing = lax.shift_right_logical(mapping, 7) == group
    landing_f = jnp.where(landing, 1.0, 0.0)
    square = (ROWS, ROWS)
    before = jnp.where(iota(square, 0) < iota(square, 1), 1.0, 0.0).astype(BF16)
    slot = dot_nn(landing_f.astype(BF16), before)
    code = iota((N_DP, ROWS), 0).astype(F32) * CAP + slot
    place = jnp.where(landing, mapping & (ROWS - 1), ROWS)
    row_of = iota(square, 0)
    total = jnp.zeros(square, F32)
    for i in range(N_DP):
        total = total + jnp.where(row_of == place[i : i + 1], code[i : i + 1], 0.0)
    codes = jnp.broadcast_to(jnp.sum(total, axis=1, keepdims=True), square).T
    for k, out_ref in enumerate(out_refs):
        out_ref[:ROWS] = grad_ref[:, head_columns(lax.axis_index("h") ^ k)]
        out_ref[ROWS:] = codes[:CHUNK].astype(BF16)


def chunk_row(code, half):
    return (code >> 3) * CHUNK + half * CAP + (code & (CAP - 1))


def code_across(side_ref):
    return side_ref[ROWS : ROWS + CHUNK].astype(F32)[0:1]


def both_halves(code, axis):
    return jnp.concatenate([chunk_row(code, half) for half in range(2)], axis=axis)


def pick_down(code):
    lane = iota((2 * ROWS, N_DP * CHUNK), 1)
    return jnp.where(lane == both_halves(code, 0), 1.0, 0.0).astype(BF16)


def code_of_block(c, head, sides):
    code = jnp.zeros((1, ROWS), F32)
    for k, side_ref in enumerate(sides):
        code = jnp.where((head ^ k) == c, code_across(side_ref), code)
    return code


def unpack_kernel(
    s0, s2, s3, s1, arrived_ref, gate_ref, query_ref, vk_ref,
):
    for c in range(HEADS):
        rows = slice(c * ROWS, (c + 1) * ROWS)
        code = code_of_block(c, lax.axis_index("h"), (s0, s1, s2, s3))
        code = jnp.broadcast_to(code, (ROWS, ROWS)).T.astype(jnp.int32)
        chunks = arrived_ref[:, c].reshape(N_DP * CHUNK, 2 * HEAD_DIM)
        moved = dot_nn(pick_down(code[:, 0:1]), chunks).astype(BF16)
        gate_ref[rows] = moved[:ROWS, :HEAD_DIM]
        vk_ref[rows, :HEAD_DIM] = moved[:ROWS, HEAD_DIM:]
        query_ref[rows] = moved[ROWS:, :HEAD_DIM]
        vk_ref[rows, HEAD_DIM:] = moved[ROWS:, HEAD_DIM:]


def gates(scores, allowed):
    half = scores * (0.5 * SCALE)
    return jnp.where(allowed, 0.5 + 0.5 * jnp.tanh(half), 0.0), half + half


def low_down(low_ref):
    return jnp.concatenate([low_ref[...]] * (STEP // ROWS), axis=1)


def pairs_allowed(key_pos, query_pos, low):
    return (key_pos >= low) & (key_pos <= query_pos)


def steps_of(parts, quarters):
    for part, quarter in zip(parts, quarters):
        for at in range(0, PART, STEP):
            yield part, slice(at, at + STEP), quarter * PART + at


def forward_kernel(
    low_ref, s0, s2, s3, s1, gate_ref, query_ref, vk1_ref, vk2_ref, vk0_ref,
    mixed_ref, gate_grad_ref, l0, l1, l2, l3, held,
):
    low = low_down(low_ref)
    quarter = lax.axis_index("x")
    query_pos = quarter * PART + iota((PART, 1), 0)
    queries = query_ref[...]
    mixed_sum = jnp.zeros((PART, HEAD_DIM), F32)
    for vk_ref, rows, at in steps_of(
        (vk2_ref, vk1_ref, vk0_ref), (quarter - 2, quarter - 1, quarter)
    ):
        allowed = pairs_allowed(at + iota((1, STEP), 1), query_pos, low)
        part, scores = gates(dot_nt(queries, vk_ref[rows, HEAD_DIM:]), allowed)
        weights = (scores * part).astype(BF16)
        mixed_sum = mixed_sum + dot_nn(weights, vk_ref[rows, :HEAD_DIM])
    center = mixed_sum - jnp.mean(mixed_sum, axis=-1, keepdims=True)
    inverse = lax.rsqrt(jnp.mean(center * center, axis=-1, keepdims=True) + EPSILON)
    normed = center * inverse
    gating = gate_ref[...].astype(F32)
    head = lax.axis_index("h")
    for k, part in enumerate((s0, s1, s2, s3)):
        held[block_rows(head ^ k), HEAD_DIM:] = part[:ROWS]
    upstream = held[:, HEAD_DIM:].astype(F32)
    layer = (normed * gating).astype(BF16)
    grad_normed = upstream * gating
    mixed_ref[...] = (
        (
            grad_normed
            - jnp.mean(grad_normed, axis=-1, keepdims=True)
            - normed * jnp.mean(grad_normed * normed, axis=-1, keepdims=True)
        )
        * inverse
    ).astype(BF16)
    gate_grad_ref[...] = (upstream * normed).astype(BF16)
    held[:, :HEAD_DIM] = layer
    for k, layer_ref in enumerate((l0, l1, l2, l3)):
        layer_ref[...] = held[block_rows(head ^ k), :HEAD_DIM]


def key_gates(keys, key_pos, queries, query_pos, low):
    part, scores = gates(dot_nt(keys, queries), pairs_allowed(key_pos, query_pos, low))
    weights = scores * part
    return weights.astype(BF16), part * (1.0 + scores - weights)


def key_grads(weights, slope, values, queries, grad_mixed):
    grad_scores = (dot_nt(values, grad_mixed) * slope).astype(BF16)
    return dot_nn(weights, grad_mixed), dot_nn(grad_scores, queries)


def query_grad_kernel(
    low_ref, low_rows_ref, s0, s2, s3, s1, mixed_ref, gate_grad_ref, query_ref, q1_ref,
    vk1_ref, vk2_ref, vk0_ref, out_ref, own_ref, picks_ref, weights_ref, slope_ref, done,
):
    low = low_down(low_ref)
    quarter = lax.axis_index("x")
    own_pos = quarter * PART + iota((PART, 1), 0)
    queries = query_ref[...]
    grad_mixed = mixed_ref[...]
    total = jnp.zeros((PART, HEAD_DIM), F32)
    for vk_ref, rows, at in steps_of(
        (vk2_ref, vk1_ref, vk0_ref), (quarter - 2, quarter - 1, quarter)
    ):
        keys = vk_ref[rows, HEAD_DIM:]
        allowed = pairs_allowed(at + iota((1, STEP), 1), own_pos, low)
        part, scores = gates(dot_nt(queries, keys), allowed)
        slope = part * (1.0 + scores - scores * part)
        grad_scores = (dot_nt(grad_mixed, vk_ref[rows, :HEAD_DIM]) * slope).astype(BF16)
        total = total + dot_nn(grad_scores, keys)
    done[0] = gate_grad_ref[...]
    done[1] = (total * SCALE).astype(BF16)
    back_picks((s0, s1, s2, s3), picks_ref)
    pack_back(picks_ref, done, out_ref, 0)
    values, keys = vk0_ref[:, :HEAD_DIM], vk0_ref[:, HEAD_DIM:]
    sums = (0.0, 0.0)
    for part, rows, at in steps_of((query_ref,), (quarter,)):
        weights, slope = key_gates(
            keys, own_pos, part[rows], at + iota((1, STEP), 1), low_rows_ref[0:1, rows]
        )
        terms = key_grads(weights, slope, values, part[rows], mixed_ref[rows])
        sums = tuple(a + b for a, b in zip(sums, terms))
    for n in range(2):
        own_ref[n] = sums[n]
    for n, (part, rows, at) in enumerate(steps_of((q1_ref,), (quarter + 1,))):
        along = PART + n * STEP
        weights_ref[n], slope_ref[n] = key_gates(
            keys, own_pos, part[rows], at + iota((1, STEP), 1),
            low_rows_ref[0:1, along : along + STEP],
        )


def back_picks(sides, picks_ref):
    sublane = iota((N_DP * CHUNK, 2 * ROWS), 0)
    for k, side_ref in enumerate(sides):
        at = both_halves(code_across(side_ref).astype(jnp.int32), 1)
        picks_ref[lax.axis_index("h") ^ k] = jnp.where(sublane == at, 1.0, 0.0).astype(BF16)


def pack_back(picks_ref, done, out_ref, j, finished=lambda c: None):
    for c in range(HEADS):
        rows = slice(c * ROWS, (c + 1) * ROWS)
        both = jnp.concatenate([done[0, rows], done[1, rows]], axis=0)
        out_ref[:, c, :, j * HEAD_DIM : (j + 1) * HEAD_DIM] = (
            dot_nn(picks_ref[c], both).astype(BF16).reshape(N_DP, CHUNK, HEAD_DIM)
        )
        finished(c)


def backward_kernel(
    low_rows_ref, picks_ref, vk_ref, q2_ref, q1_ref, m2_ref, m1_ref,
    own_ref, weights_ref, slope_ref, gq_ref, out_ref, done, packed, sems,
):
    packed[:, :, :, :HEAD_DIM] = gq_ref[...]
    quarter = lax.axis_index("x")
    own_pos = quarter * PART + iota((PART, 1), 0)
    values, keys = vk_ref[:, :HEAD_DIM], vk_ref[:, HEAD_DIM:]
    sums = (own_ref[0], own_ref[1])
    later = steps_of(((q1_ref, m1_ref), (q2_ref, m2_ref)), (quarter + 1, quarter + 2))
    for n, ((part, mixed), rows, at) in enumerate(later):
        along = PART + n * STEP
        if n < PART // STEP:
            weights, slope = weights_ref[n], slope_ref[n]
        else:
            weights, slope = key_gates(
                keys, own_pos, part[rows], at + iota((1, STEP), 1),
                low_rows_ref[0:1, along : along + STEP],
            )
        terms = key_grads(weights, slope, values, part[rows], mixed[rows])
        sums = tuple(a + b for a, b in zip(sums, terms))
    done[0] = sums[0].astype(BF16)
    done[1] = (sums[1] * SCALE).astype(BF16)
    stores = []

    def send(c):
        stores.append(pltpu.make_async_copy(packed.at[:, c], out_ref.at[:, c], sems.at[c]))
        stores[-1].start()

    pack_back(picks_ref, done, packed, 1, send)
    for store in stores:
        store.wait()


def finish_kernel(
    home_ref, l0, l2, l3, l1, back_ref, grad_ref, out_ref, grads, sems
):
    stores = []
    for k, layer_ref in enumerate((l0, l1, l2, l3)):
        columns = head_columns(lax.axis_index("h") ^ k)
        stores.append(pltpu.make_async_copy(layer_ref, out_ref.at[:, columns], sems.at[k]))
        stores[-1].start()
    pick = home_ref[...]
    for h in range(HEADS):
        chunks = back_ref[:, h].reshape(N_DP * CHUNK, 2 * HEAD_DIM)
        moved = dot_nn(pick, chunks).astype(BF16)
        for half in range(2):
            for j in range(2):
                block = 2 * half + j
                at = (block * HEADS + h) * HEAD_DIM
                columns = slice(at, at + HEAD_DIM)
                grads[:, columns] = moved[
                    half * ROWS : (half + 1) * ROWS, j * HEAD_DIM : (j + 1) * HEAD_DIM
                ]
                stores.append(
                    pltpu.make_async_copy(
                        grads.at[:, columns], grad_ref.at[:, columns], sems.at[HEADS + 4 * h + block]
                    )
                )
                stores[-1].start()
    for store in stores:
        store.wait()


def route(chunks):
    flat = chunks.reshape(N_DP * HEADS * CHUNK, 2 * HEAD_DIM)
    moved = lax.all_to_all(flat, ("dp", "h"), 0, 0, tiled=True)
    return moved.reshape(chunks.shape)


def from_quarter(array, by):
    pairs = [(i, i - by) for i in range(N_X) if 0 <= i - by < N_X]
    return lax.ppermute(array, "x", pairs)


def swap_heads(pieces):
    return [pieces[0]] + [
        lax.ppermute(pieces[k], "h", [(i, i ^ k) for i in range(HEADS)]) for k in (2, 3, 1)
    ]


def body(projected, destination, lengths, grad_out):
    mapping = destination.reshape(N_DP, ROWS)
    chunked = shape(N_DP, HEADS, CHUNK, 2 * HEAD_DIM)
    half_chunked = shape(N_DP, HEADS, CHUNK, HEAD_DIM)
    head_part = shape(PART, HEAD_DIM)
    pieces = [shape(ROWS, HEAD_DIM)] * HEADS
    dma = pltpu.SemaphoreType.DMA
    (packed,) = call(
        pack_kernel, [chunked], (mapping, projected),
        scratch=[
            pltpu.VMEM(projected.shape, BF16), pltpu.VMEM(chunked.shape, BF16), dma, dma((2,)),
        ],
        flops=2 * 256 * 128 * 2048, nbytes=3 << 19,
        hbm_in=(1,), hbm_out=True, limit=62 * 1024 * 1024,
    )
    *side_out, home, low, low_rows = call(
        side_kernel,
        [shape(ROWS + CHUNK, HEAD_DIM)] * HEADS
        + [
            shape(2 * ROWS, N_DP * CHUNK), shape(PART, ROWS, dtype=jnp.int32),
            shape(8, (REACH + 1) * PART, dtype=jnp.int32),
        ],
        (lengths, mapping, grad_out), smem=(0,), nbytes=3 << 17,
    )
    side = swap_heads(side_out)
    arrived = route(packed)
    gate, queries, vk = call(
        unpack_kernel, [head_part, head_part, shape(PART, 2 * HEAD_DIM)], (*side, arrived),
        flops=1 << 28, nbytes=2 << 20,
    )
    vk_parts = (from_quarter(vk, -1), from_quarter(vk, -2), vk)
    query_parts = (from_quarter(queries, 2), from_quarter(queries, 1))
    held = pltpu.VMEM((PART, 2 * HEAD_DIM), BF16)
    done = pltpu.VMEM((2, PART, HEAD_DIM), BF16)
    mixed, gate_grad, *layer = call(
        forward_kernel, [head_part, head_part, *pieces],
        (low, *side, gate, queries, *vk_parts),
        scratch=[held], flops=1 << 29, nbytes=2 << 20,
    )
    mixed_parts = (from_quarter(mixed, 2), from_quarter(mixed, 1))
    layer_home = swap_heads(layer)
    gq_back, own, picks, weights, slopes = call(
        query_grad_kernel,
        [half_chunked, shape(2, PART, HEAD_DIM, dtype=F32), shape(HEADS, N_DP * CHUNK, 2 * ROWS),
         shape(PART // STEP, PART, STEP), shape(PART // STEP, PART, STEP, dtype=F32)],
        (low, low_rows, *side, mixed, gate_grad, queries, query_parts[1], *vk_parts),
        scratch=[done], flops=1 << 29, nbytes=2 << 20,
    )
    (back,) = call(
        backward_kernel, [chunked],
        (low_rows, picks, vk, *query_parts, *mixed_parts, own, weights, slopes, gq_back),
        scratch=[done, pltpu.VMEM(chunked.shape, BF16), dma((HEADS,))],
        flops=1 << 30, nbytes=3 << 20, hbm_out=True,
    )
    returned = route(back)
    grad_projected, layer_output = call(
        finish_kernel, [shape(ROWS, 4 * HEADS * HEAD_DIM), shape(ROWS, HEADS * HEAD_DIM)],
        (home, *layer_home, returned),
        scratch=[pltpu.VMEM(projected.shape, BF16), dma((5 * HEADS,))],
        flops=1 << 28, nbytes=2 << 20, hbm_out=True,
    )
    return (layer_output, grad_projected)


def solution(mesh):
    fine = Mesh(mesh.devices.reshape(N_DP, N_X, HEADS), ("dp", "x", "h"))
    rows = P(("dp", "x", "h"), None)
    in_specs = (rows, P(("x", "h"), None), P("dp", None), rows)
    return jax.shard_map(
        body, mesh=fine, in_specs=in_specs, out_specs=(rows, rows), check_vma=False
    )
```

```python
import functools

import jax
import jax.numpy as jnp
from jax import lax
from jax.experimental import pallas as pl
from jax.experimental.pallas import tpu as pltpu
from jax.sharding import Mesh
from jax.sharding import PartitionSpec as P

HEADS = 4
HEAD_DIM = 128
BLOCK = 128
USERS = 3
EPSILON = 1e-06
SCALE = HEAD_DIM ** (-0.5)
ROWS = 128
CAP = 8
N_DP = 32
N_X = 4
REACH = 2
PART = HEADS * ROWS
GROUP = N_X * PART
STEP = 256
VMEM_LIMIT = 48 * 1024 * 1024
CHUNK = 2 * CAP

F32 = jnp.float32
BF16 = jnp.bfloat16


def dot_nn(a, b):
    return lax.dot_general(a, b, (((1,), (0,)), ((), ())), preferred_element_type=F32)


def dot_nt(a, b):
    return lax.dot_general(a, b, (((1,), (1,)), ((), ())), preferred_element_type=F32)


def iota(shape, dim):
    return lax.broadcasted_iota(jnp.int32, shape, dim)


def call(kernel, outs, ins, smem=(), scratch=(), flops=0, nbytes=0, hbm_in=(), hbm_out=False, limit=VMEM_LIMIT):
    spaces = [pltpu.VMEM] * len(ins)
    for n in smem:
        spaces[n] = pltpu.SMEM
    for n in hbm_in:
        spaces[n] = pl.ANY
    return pl.pallas_call(
        kernel,
        out_shape=outs,
        in_specs=[pl.BlockSpec(memory_space=space) for space in spaces],
        out_specs=[pl.BlockSpec(memory_space=pl.ANY if hbm_out else pltpu.VMEM)] * len(outs),
        scratch_shapes=list(scratch),
        compiler_params=pltpu.CompilerParams(vmem_limit_bytes=limit),
        name=kernel.__name__,
        cost_estimate=pl.CostEstimate(flops=flops, bytes_accessed=nbytes, transcendentals=0),
    )(*ins)


def shape(*dims, dtype=BF16):
    return jax.ShapeDtypeStruct(dims, dtype)


def owners_of(dest_ref, dp):
    targets = dest_ref[pl.ds(dp, 1), :]
    owners = lax.shift_right_logical(targets, 7).astype(F32)
    across = jnp.broadcast_to(owners, (ROWS, ROWS))
    return across, across.T


def pack_kernel(dest_ref, proj_ref, out_ref, proj, packed, in_sem, out_sems):
    load = pltpu.make_async_copy(proj_ref, proj, in_sem)
    load.start()
    across, down = owners_of(dest_ref, lax.axis_index("dp"))
    square = (ROWS, ROWS)
    earlier = (across == down) & (iota(square, 0) < iota(square, 1))
    slot = jnp.sum(jnp.where(earlier, 1.0, 0.0), axis=0, keepdims=True)
    key = (across[0:1] * CAP + slot).astype(jnp.int32)
    pick = jnp.where(iota((N_DP * CAP, ROWS), 0) == key, 1.0, 0.0).astype(BF16)
    load.wait()
    stores = []
    for pair in range(0, HEADS, 2):
        for j in range(2):
            halves = []
            for block in (j, 2 + j):
                at = (block * HEADS + pair) * HEAD_DIM
                moved = dot_nn(pick, proj[:, at : at + 2 * HEAD_DIM])
                halves.append(moved.reshape(N_DP, CAP, 2 * HEAD_DIM))
            chunks = jnp.concatenate(halves, axis=1).astype(BF16)
            for h in range(2):
                packed[:, pair + h, :, j * HEAD_DIM : (j + 1) * HEAD_DIM] = chunks[
                    :, :, h * HEAD_DIM : (h + 1) * HEAD_DIM
                ]
        heads = slice(pair, pair + 2)
        stores.append(
            pltpu.make_async_copy(packed.at[:, heads], out_ref.at[:, heads], out_sems.at[pair // 2])
        )
        stores[-1].start()
    for store in stores:
        store.wait()


def head_columns(h):
    return pl.ds(pl.multiple_of(h * HEAD_DIM, HEAD_DIM), HEAD_DIM)


def block_rows(c):
    return pl.ds(pl.multiple_of(c * ROWS, ROWS), ROWS)


def user_bounds(lengths_ref):
    bounds, start = [], jnp.int32(0)
    for u in range(USERS):
        length = lengths_ref[0, u]
        padded = (length + BLOCK - 1) // BLOCK * BLOCK
        bounds.append((start, start + length, start + padded))
        start = start + padded
    return bounds


def first_key(positions, bounds):
    low = jnp.full(positions.shape, 2 * GROUP, jnp.int32)
    for start, end, _ in bounds:
        low = jnp.where((positions >= start) & (positions < end), start, low)
    return low


def side_kernel(lengths_ref, dest_ref, grad_ref, *out_refs):
    *out_refs, code_ref, home_ref, low_ref, low_rows_ref = out_refs
    bounds = user_bounds(lengths_ref)
    base = lax.axis_index("x") * PART
    low_ref[...] = first_key(base + iota(low_ref.shape, 0), bounds)
    low_rows_ref[...] = first_key(base + iota(low_rows_ref.shape, 1), bounds)
    across, down = owners_of(dest_ref, lax.axis_index("dp"))
    earlier = (across == down) & (iota((ROWS, ROWS), 1) < iota((ROWS, ROWS), 0))
    rank = jnp.sum(jnp.where(earlier, 1.0, 0.0), axis=1, keepdims=True)
    home_ref[...] = pick_down((down[:, 0:1] * CAP + rank).astype(jnp.int32))
    group = lax.axis_index("dp")
    mapping = dest_ref[...]
    landing = lax.shift_right_logical(mapping, 7) == group
    landing_f = jnp.where(landing, 1.0, 0.0)
    square = (ROWS, ROWS)
    before = jnp.where(iota(square, 0) < iota(square, 1), 1.0, 0.0).astype(BF16)
    slot = dot_nn(landing_f.astype(BF16), before)
    code = iota((N_DP, ROWS), 0).astype(F32) * CAP + slot
    place = jnp.where(landing, mapping & (ROWS - 1), ROWS)
    row_of = iota(square, 0)
    total = jnp.zeros(square, F32)
    for i in range(N_DP):
        total = total + jnp.where(row_of == place[i : i + 1], code[i : i + 1], 0.0)
    codes = jnp.broadcast_to(jnp.sum(total, axis=1, keepdims=True), square).T
    for k, out_ref in enumerate(out_refs):
        out_ref[...] = grad_ref[:, head_columns(lax.axis_index("h") ^ k)]
    code_ref[...] = codes[0:1]


def chunk_row(code, half):
    return (code >> 3) * CHUNK + half * CAP + (code & (CAP - 1))


def both_halves(code, axis):
    return jnp.concatenate([chunk_row(code, half) for half in range(2)], axis=axis)


def pick_down(code):
    lane = iota((2 * ROWS, N_DP * CHUNK), 1)
    return jnp.where(lane == both_halves(code, 0), 1.0, 0.0).astype(BF16)


def code_of_block(c, head, sides):
    code = jnp.zeros((1, ROWS), F32)
    for k, side_ref in enumerate(sides):
        code = jnp.where((head ^ k) == c, side_ref[...], code)
    return code


def unpack_kernel(
    g0, g2, g3, g1, s0, s2, s3, s1, arrived_ref, gate_ref, query_ref, vk_ref,
):
    del g0, g2, g3, g1
    for c in range(HEADS):
        rows = slice(c * ROWS, (c + 1) * ROWS)
        code = code_of_block(c, lax.axis_index("h"), (s0, s1, s2, s3))
        code = jnp.broadcast_to(code, (ROWS, ROWS)).T.astype(jnp.int32)
        chunks = arrived_ref[:, c].reshape(N_DP * CHUNK, 2 * HEAD_DIM)
        moved = dot_nn(pick_down(code[:, 0:1]), chunks).astype(BF16)
        gate_ref[rows] = moved[:ROWS, :HEAD_DIM]
        vk_ref[rows, :HEAD_DIM] = moved[:ROWS, HEAD_DIM:]
        query_ref[rows] = moved[ROWS:, :HEAD_DIM]
        vk_ref[rows, HEAD_DIM:] = moved[ROWS:, HEAD_DIM:]


def gates(scores, allowed):
    half = scores * (0.5 * SCALE)
    return jnp.where(allowed, 0.5 + 0.5 * jnp.tanh(half), 0.0), half + half


def low_down(low_ref):
    return jnp.concatenate([low_ref[...]] * (STEP // ROWS), axis=1)


def pairs_allowed(key_pos, query_pos, low):
    return (key_pos >= low) & (key_pos <= query_pos)


def steps_of(parts, quarters):
    for part, quarter in zip(parts, quarters):
        for at in range(0, PART, STEP):
            yield part, slice(at, at + STEP), quarter * PART + at


def forward_kernel(
    low_ref, s0, s2, s3, s1, gate_ref, query_ref, vk1_ref, vk2_ref, vk0_ref,
    mixed_ref, gate_grad_ref, l0, l1, l2, l3, held,
):
    low = low_down(low_ref)
    quarter = lax.axis_index("x")
    query_pos = quarter * PART + iota((PART, 1), 0)
    queries = query_ref[...]
    mixed_sum = jnp.zeros((PART, HEAD_DIM), F32)
    for vk_ref, rows, at in steps_of(
        (vk2_ref, vk1_ref, vk0_ref), (quarter - 2, quarter - 1, quarter)
    ):
        allowed = pairs_allowed(at + iota((1, STEP), 1), query_pos, low)
        part, scores = gates(dot_nt(queries, vk_ref[rows, HEAD_DIM:]), allowed)
        weights = (scores * part).astype(BF16)
        mixed_sum = mixed_sum + dot_nn(weights, vk_ref[rows, :HEAD_DIM])
    center = mixed_sum - jnp.mean(mixed_sum, axis=-1, keepdims=True)
    inverse = lax.rsqrt(jnp.mean(center * center, axis=-1, keepdims=True) + EPSILON)
    normed = center * inverse
    gating = gate_ref[...].astype(F32)
    head = lax.axis_index("h")
    for k, part in enumerate((s0, s1, s2, s3)):
        held[block_rows(head ^ k), HEAD_DIM:] = part[...]
    upstream = held[:, HEAD_DIM:].astype(F32)
    layer = (normed * gating).astype(BF16)
    grad_normed = upstream * gating
    mixed_ref[...] = (
        (
            grad_normed
            - jnp.mean(grad_normed, axis=-1, keepdims=True)
            - normed * jnp.mean(grad_normed * normed, axis=-1, keepdims=True)
        )
        * inverse
    ).astype(BF16)
    gate_grad_ref[...] = (upstream * normed).astype(BF16)
    held[:, :HEAD_DIM] = layer
    for k, layer_ref in enumerate((l0, l1, l2, l3)):
        layer_ref[...] = held[block_rows(head ^ k), :HEAD_DIM]


def key_gates(keys, key_pos, queries, query_pos, low):
    part, scores = gates(dot_nt(keys, queries), pairs_allowed(key_pos, query_pos, low))
    weights = scores * part
    return weights.astype(BF16), part * (1.0 + scores - weights)


def key_grads(weights, slope, values, queries, grad_mixed):
    grad_scores = (dot_nt(values, grad_mixed) * slope).astype(BF16)
    return dot_nn(weights, grad_mixed), dot_nn(grad_scores, queries)


def query_grad_kernel(
    low_ref, low_rows_ref, s0, s2, s3, s1, mixed_ref, gate_grad_ref, query_ref, q1_ref,
    vk1_ref, vk2_ref, vk0_ref, out_ref, own_ref, picks_ref, weights_ref, slope_ref, done,
):
    low = low_down(low_ref)
    quarter = lax.axis_index("x")
    own_pos = quarter * PART + iota((PART, 1), 0)
    queries = query_ref[...]
    grad_mixed = mixed_ref[...]
    total = jnp.zeros((PART, HEAD_DIM), F32)
    for vk_ref, rows, at in steps_of(
        (vk2_ref, vk1_ref, vk0_ref), (quarter - 2, quarter - 1, quarter)
    ):
        keys = vk_ref[rows, HEAD_DIM:]
        allowed = pairs_allowed(at + iota((1, STEP), 1), own_pos, low)
        part, scores = gates(dot_nt(queries, keys), allowed)
        slope = part * (1.0 + scores - scores * part)
        grad_scores = (dot_nt(grad_mixed, vk_ref[rows, :HEAD_DIM]) * slope).astype(BF16)
        total = total + dot_nn(grad_scores, keys)
    done[0] = gate_grad_ref[...]
    done[1] = (total * SCALE).astype(BF16)
    back_picks((s0, s1, s2, s3), picks_ref)
    pack_back(picks_ref, done, out_ref, 0)
    values, keys = vk0_ref[:, :HEAD_DIM], vk0_ref[:, HEAD_DIM:]
    sums = (0.0, 0.0)
    for part, rows, at in steps_of((query_ref,), (quarter,)):
        weights, slope = key_gates(
            keys, own_pos, part[rows], at + iota((1, STEP), 1), low_rows_ref[0:1, rows]
        )
        terms = key_grads(weights, slope, values, part[rows], mixed_ref[rows])
        sums = tuple(a + b for a, b in zip(sums, terms))
    for n in range(2):
        own_ref[n] = sums[n]
    for n, (part, rows, at) in enumerate(steps_of((q1_ref,), (quarter + 1,))):
        along = PART + n * STEP
        weights_ref[n], slope_ref[n] = key_gates(
            keys, own_pos, part[rows], at + iota((1, STEP), 1),
            low_rows_ref[0:1, along : along + STEP],
        )


def back_picks(sides, picks_ref):
    sublane = iota((N_DP * CHUNK, 2 * ROWS), 0)
    for k, side_ref in enumerate(sides):
        at = both_halves(side_ref[...].astype(jnp.int32), 1)
        picks_ref[lax.axis_index("h") ^ k] = jnp.where(sublane == at, 1.0, 0.0).astype(BF16)


def pack_back(picks_ref, done, out_ref, j, finished=lambda c: None):
    for c in range(HEADS):
        rows = slice(c * ROWS, (c + 1) * ROWS)
        both = jnp.concatenate([done[0, rows], done[1, rows]], axis=0)
        out_ref[:, c, :, j * HEAD_DIM : (j + 1) * HEAD_DIM] = (
            dot_nn(picks_ref[c], both).astype(BF16).reshape(N_DP, CHUNK, HEAD_DIM)
        )
        finished(c)


def backward_kernel(
    low_rows_ref, picks_ref, vk_ref, q2_ref, q1_ref, m2_ref, m1_ref,
    own_ref, weights_ref, slope_ref, gq_ref, out_ref, done, packed, sems,
):
    packed[:, :, :, :HEAD_DIM] = gq_ref[...]
    quarter = lax.axis_index("x")
    own_pos = quarter * PART + iota((PART, 1), 0)
    values, keys = vk_ref[:, :HEAD_DIM], vk_ref[:, HEAD_DIM:]
    sums = (own_ref[0], own_ref[1])
    later = steps_of(((q1_ref, m1_ref), (q2_ref, m2_ref)), (quarter + 1, quarter + 2))
    for n, ((part, mixed), rows, at) in enumerate(later):
        along = PART + n * STEP
        if n < PART // STEP:
            weights, slope = weights_ref[n], slope_ref[n]
        else:
            weights, slope = key_gates(
                keys, own_pos, part[rows], at + iota((1, STEP), 1),
                low_rows_ref[0:1, along : along + STEP],
            )
        terms = key_grads(weights, slope, values, part[rows], mixed[rows])
        sums = tuple(a + b for a, b in zip(sums, terms))
    done[0] = sums[0].astype(BF16)
    done[1] = (sums[1] * SCALE).astype(BF16)
    stores = []

    def send(c):
        stores.append(pltpu.make_async_copy(packed.at[:, c], out_ref.at[:, c], sems.at[c]))
        stores[-1].start()

    pack_back(picks_ref, done, packed, 1, send)
    for store in stores:
        store.wait()


def finish_kernel(
    home_ref, l0, l2, l3, l1, back_ref, grad_ref, out_ref, grads, sems
):
    stores = []
    for k, layer_ref in enumerate((l0, l1, l2, l3)):
        columns = head_columns(lax.axis_index("h") ^ k)
        stores.append(pltpu.make_async_copy(layer_ref, out_ref.at[:, columns], sems.at[k]))
        stores[-1].start()
    pick = home_ref[...]
    for h in range(HEADS):
        chunks = back_ref[:, h].reshape(N_DP * CHUNK, 2 * HEAD_DIM)
        moved = dot_nn(pick, chunks).astype(BF16)
        for half in range(2):
            for j in range(2):
                block = 2 * half + j
                at = (block * HEADS + h) * HEAD_DIM
                columns = slice(at, at + HEAD_DIM)
                grads[:, columns] = moved[
                    half * ROWS : (half + 1) * ROWS, j * HEAD_DIM : (j + 1) * HEAD_DIM
                ]
                stores.append(
                    pltpu.make_async_copy(
                        grads.at[:, columns], grad_ref.at[:, columns], sems.at[HEADS + 4 * h + block]
                    )
                )
                stores[-1].start()
    for store in stores:
        store.wait()


def route(chunks):
    flat = chunks.reshape(N_DP * HEADS * CHUNK, 2 * HEAD_DIM)
    moved = lax.all_to_all(flat, ("dp", "h"), 0, 0, tiled=True)
    return moved.reshape(chunks.shape)


def from_quarter(array, by):
    pairs = [(i, i - by) for i in range(N_X) if 0 <= i - by < N_X]
    return lax.ppermute(array, "x", pairs)


def swap_heads(pieces):
    return [pieces[0]] + [
        lax.ppermute(pieces[k], "h", [(i, i ^ k) for i in range(HEADS)]) for k in (2, 3, 1)
    ]


def body(projected, destination, lengths, grad_out):
    mapping = destination.reshape(N_DP, ROWS)
    chunked = shape(N_DP, HEADS, CHUNK, 2 * HEAD_DIM)
    half_chunked = shape(N_DP, HEADS, CHUNK, HEAD_DIM)
    head_part = shape(PART, HEAD_DIM)
    pieces = [shape(ROWS, HEAD_DIM)] * HEADS
    dma = pltpu.SemaphoreType.DMA
    (packed,) = call(
        pack_kernel, [chunked], (mapping, projected),
        scratch=[
            pltpu.VMEM(projected.shape, BF16), pltpu.VMEM(chunked.shape, BF16), dma, dma((2,)),
        ],
        flops=2 * 256 * 128 * 2048, nbytes=3 << 19,
        hbm_in=(1,), hbm_out=True, limit=62 * 1024 * 1024,
    )
    *side_out, code, home, low, low_rows = call(
        side_kernel,
        pieces
        + [
            shape(1, ROWS, dtype=F32),
            shape(2 * ROWS, N_DP * CHUNK), shape(PART, ROWS, dtype=jnp.int32),
            shape(8, (REACH + 1) * PART, dtype=jnp.int32),
        ],
        (lengths, mapping, grad_out), smem=(0,), nbytes=3 << 17,
    )
    side = swap_heads(side_out)
    codes = swap_heads([code] * HEADS)
    arrived = route(packed)
    gate, queries, vk = call(
        unpack_kernel, [head_part, head_part, shape(PART, 2 * HEAD_DIM)], (*side, *codes, arrived),
        hbm_in=(0, 1, 2, 3),
        flops=1 << 28, nbytes=2 << 20,
    )
    vk_parts = (from_quarter(vk, -1), from_quarter(vk, -2), vk)
    query_parts = (from_quarter(queries, 2), from_quarter(queries, 1))
    held = pltpu.VMEM((PART, 2 * HEAD_DIM), BF16)
    done = pltpu.VMEM((2, PART, HEAD_DIM), BF16)
    mixed, gate_grad, *layer = call(
        forward_kernel, [head_part, head_part, *pieces],
        (low, *side, gate, queries, *vk_parts),
        scratch=[held], flops=1 << 29, nbytes=2 << 20,
    )
    mixed_parts = (from_quarter(mixed, 2), from_quarter(mixed, 1))
    layer_home = swap_heads(layer)
    gq_back, own, picks, weights, slopes = call(
        query_grad_kernel,
        [half_chunked, shape(2, PART, HEAD_DIM, dtype=F32), shape(HEADS, N_DP * CHUNK, 2 * ROWS),
         shape(PART // STEP, PART, STEP), shape(PART // STEP, PART, STEP, dtype=F32)],
        (low, low_rows, *codes, mixed, gate_grad, queries, query_parts[1], *vk_parts),
        scratch=[done], flops=1 << 29, nbytes=2 << 20,
    )
    (back,) = call(
        backward_kernel, [chunked],
        (low_rows, picks, vk, *query_parts, *mixed_parts, own, weights, slopes, gq_back),
        scratch=[done, pltpu.VMEM(chunked.shape, BF16), dma((HEADS,))],
        flops=1 << 30, nbytes=3 << 20, hbm_out=True,
    )
    returned = route(back)
    grad_projected, layer_output = call(
        finish_kernel, [shape(ROWS, 4 * HEADS * HEAD_DIM), shape(ROWS, HEADS * HEAD_DIM)],
        (home, *layer_home, returned),
        scratch=[pltpu.VMEM(projected.shape, BF16), dma((5 * HEADS,))],
        flops=1 << 28, nbytes=2 << 20, hbm_out=True,
    )
    return (layer_output, grad_projected)


def solution(mesh):
    fine = Mesh(mesh.devices.reshape(N_DP, N_X, HEADS), ("dp", "x", "h"))
    rows = P(("dp", "x", "h"), None)
    in_specs = (rows, P(("x", "h"), None), P("dp", None), rows)
    return jax.shard_map(
        body, mesh=fine, in_specs=in_specs, out_specs=(rows, rows), check_vma=False
    )
```

```python
import functools

import jax
import jax.numpy as jnp
from jax import lax
from jax.experimental import pallas as pl
from jax.experimental.pallas import tpu as pltpu
from jax.sharding import Mesh
from jax.sharding import PartitionSpec as P

HEADS = 4
HEAD_DIM = 128
BLOCK = 128
USERS = 3
EPSILON = 1e-06
SCALE = HEAD_DIM ** (-0.5)
ROWS = 128
CAP = 8
N_DP = 32
N_X = 4
REACH = 2
PART = HEADS * ROWS
GROUP = N_X * PART
STEP = 256
VMEM_LIMIT = 48 * 1024 * 1024
CHUNK = 2 * CAP

F32 = jnp.float32
BF16 = jnp.bfloat16


def dot_nn(a, b):
    return lax.dot_general(a, b, (((1,), (0,)), ((), ())), preferred_element_type=F32)


def dot_nt(a, b):
    return lax.dot_general(a, b, (((1,), (1,)), ((), ())), preferred_element_type=F32)


def iota(shape, dim):
    return lax.broadcasted_iota(jnp.int32, shape, dim)


def call(kernel, outs, ins, smem=(), scratch=(), flops=0, nbytes=0, hbm_in=(), hbm_out=False, limit=VMEM_LIMIT):
    spaces = [pltpu.VMEM] * len(ins)
    for n in smem:
        spaces[n] = pltpu.SMEM
    for n in hbm_in:
        spaces[n] = pl.ANY
    return pl.pallas_call(
        kernel,
        out_shape=outs,
        in_specs=[pl.BlockSpec(memory_space=space) for space in spaces],
        out_specs=[pl.BlockSpec(memory_space=pl.ANY if hbm_out else pltpu.VMEM)] * len(outs),
        scratch_shapes=list(scratch),
        compiler_params=pltpu.CompilerParams(vmem_limit_bytes=limit),
        name=kernel.__name__,
        cost_estimate=pl.CostEstimate(flops=flops, bytes_accessed=nbytes, transcendentals=0),
    )(*ins)


def shape(*dims, dtype=BF16):
    return jax.ShapeDtypeStruct(dims, dtype)


def owners_of(dest_ref, dp):
    targets = dest_ref[pl.ds(dp, 1), :]
    owners = lax.shift_right_logical(targets, 7).astype(F32)
    across = jnp.broadcast_to(owners, (ROWS, ROWS))
    return across, across.T


def pack_kernel(dest_ref, proj_ref, out_ref, proj, packed, in_sem, out_sems):
    load = pltpu.make_async_copy(proj_ref, proj, in_sem)
    load.start()
    across, down = owners_of(dest_ref, lax.axis_index("dp"))
    square = (ROWS, ROWS)
    earlier = (across == down) & (iota(square, 0) < iota(square, 1))
    slot = jnp.sum(jnp.where(earlier, 1.0, 0.0), axis=0, keepdims=True)
    key = (across[0:1] * CAP + slot).astype(jnp.int32)
    pick = jnp.where(iota((N_DP * CAP, ROWS), 0) == key, 1.0, 0.0).astype(BF16)
    load.wait()
    stores = []
    for pair in range(0, HEADS, 2):
        for j in range(2):
            halves = []
            for block in (j, 2 + j):
                at = (block * HEADS + pair) * HEAD_DIM
                moved = dot_nn(pick, proj[:, at : at + 2 * HEAD_DIM])
                halves.append(moved.reshape(N_DP, CAP, 2 * HEAD_DIM))
            chunks = jnp.concatenate(halves, axis=1).astype(BF16)
            for h in range(2):
                packed[:, pair + h, :, j * HEAD_DIM : (j + 1) * HEAD_DIM] = chunks[
                    :, :, h * HEAD_DIM : (h + 1) * HEAD_DIM
                ]
        heads = slice(pair, pair + 2)
        stores.append(
            pltpu.make_async_copy(packed.at[:, heads], out_ref.at[:, heads], out_sems.at[pair // 2])
        )
        stores[-1].start()
    for store in stores:
        store.wait()


def head_columns(h):
    return pl.ds(pl.multiple_of(h * HEAD_DIM, HEAD_DIM), HEAD_DIM)


def block_rows(c):
    return pl.ds(pl.multiple_of(c * ROWS, ROWS), ROWS)


def user_bounds(lengths_ref):
    bounds, start = [], jnp.int32(0)
    for u in range(USERS):
        length = lengths_ref[0, u]
        padded = (length + BLOCK - 1) // BLOCK * BLOCK
        bounds.append((start, start + length, start + padded))
        start = start + padded
    return bounds


def first_key(positions, bounds):
    low = jnp.full(positions.shape, 2 * GROUP, jnp.int32)
    for start, end, _ in bounds:
        low = jnp.where((positions >= start) & (positions < end), start, low)
    return low


def plan_kernel(lengths_ref, dest_ref, side_ref, home_ref, low_ref, low_rows_ref):
    del side_ref
    bounds = user_bounds(lengths_ref)
    base = lax.axis_index("x") * PART
    low_ref[...] = first_key(base + iota(low_ref.shape, 0), bounds)
    low_rows_ref[...] = first_key(base + iota(low_rows_ref.shape, 1), bounds)
    across, down = owners_of(dest_ref, lax.axis_index("dp"))
    earlier = (across == down) & (iota((ROWS, ROWS), 1) < iota((ROWS, ROWS), 0))
    rank = jnp.sum(jnp.where(earlier, 1.0, 0.0), axis=1, keepdims=True)
    home_ref[...] = pick_down((down[:, 0:1] * CAP + rank).astype(jnp.int32))


def side_kernel(dest_ref, grad_ref, *out_refs):
    group = lax.axis_index("dp")
    mapping = dest_ref[...]
    landing = lax.shift_right_logical(mapping, 7) == group
    landing_f = jnp.where(landing, 1.0, 0.0)
    square = (ROWS, ROWS)
    before = jnp.where(iota(square, 0) < iota(square, 1), 1.0, 0.0).astype(BF16)
    slot = dot_nn(landing_f.astype(BF16), before)
    code = iota((N_DP, ROWS), 0).astype(F32) * CAP + slot
    place = jnp.where(landing, mapping & (ROWS - 1), ROWS)
    row_of = iota(square, 0)
    total = jnp.zeros(square, F32)
    for i in range(N_DP):
        total = total + jnp.where(row_of == place[i : i + 1], code[i : i + 1], 0.0)
    codes = jnp.broadcast_to(jnp.sum(total, axis=1, keepdims=True), square).T
    for k, out_ref in enumerate(out_refs):
        out_ref[:ROWS] = grad_ref[:, head_columns(lax.axis_index("h") ^ k)]
        out_ref[ROWS:] = codes[:CHUNK].astype(BF16)


def chunk_row(code, half):
    return (code >> 3) * CHUNK + half * CAP + (code & (CAP - 1))


def code_across(side_ref):
    return side_ref[ROWS : ROWS + CHUNK].astype(F32)[0:1]


def both_halves(code, axis):
    return jnp.concatenate([chunk_row(code, half) for half in range(2)], axis=axis)


def pick_down(code):
    lane = iota((2 * ROWS, N_DP * CHUNK), 1)
    return jnp.where(lane == both_halves(code, 0), 1.0, 0.0).astype(BF16)


def code_of_block(c, head, sides):
    code = jnp.zeros((1, ROWS), F32)
    for k, side_ref in enumerate(sides):
        code = jnp.where((head ^ k) == c, code_across(side_ref), code)
    return code


def unpack_kernel(
    s0, s2, s3, s1, arrived_ref, gate_ref, query_ref, vk_ref,
):
    for c in range(HEADS):
        rows = slice(c * ROWS, (c + 1) * ROWS)
        code = code_of_block(c, lax.axis_index("h"), (s0, s1, s2, s3))
        code = jnp.broadcast_to(code, (ROWS, ROWS)).T.astype(jnp.int32)
        chunks = arrived_ref[:, c].reshape(N_DP * CHUNK, 2 * HEAD_DIM)
        moved = dot_nn(pick_down(code[:, 0:1]), chunks).astype(BF16)
        gate_ref[rows] = moved[:ROWS, :HEAD_DIM]
        vk_ref[rows, :HEAD_DIM] = moved[:ROWS, HEAD_DIM:]
        query_ref[rows] = moved[ROWS:, :HEAD_DIM]
        vk_ref[rows, HEAD_DIM:] = moved[ROWS:, HEAD_DIM:]


def gates(scores, allowed):
    half = scores * (0.5 * SCALE)
    return jnp.where(allowed, 0.5 + 0.5 * jnp.tanh(half), 0.0), half + half


def low_down(low_ref):
    return jnp.concatenate([low_ref[...]] * (STEP // ROWS), axis=1)


def pairs_allowed(key_pos, query_pos, low):
    return (key_pos >= low) & (key_pos <= query_pos)


def steps_of(parts, quarters):
    for part, quarter in zip(parts, quarters):
        for at in range(0, PART, STEP):
            yield part, slice(at, at + STEP), quarter * PART + at


def forward_kernel(
    low_ref, s0, s2, s3, s1, gate_ref, query_ref, vk1_ref, vk2_ref, vk0_ref,
    mixed_ref, gate_grad_ref, l0, l1, l2, l3, held,
):
    low = low_down(low_ref)
    quarter = lax.axis_index("x")
    query_pos = quarter * PART + iota((PART, 1), 0)
    queries = query_ref[...]
    mixed_sum = jnp.zeros((PART, HEAD_DIM), F32)
    for vk_ref, rows, at in steps_of(
        (vk2_ref, vk1_ref, vk0_ref), (quarter - 2, quarter - 1, quarter)
    ):
        allowed = pairs_allowed(at + iota((1, STEP), 1), query_pos, low)
        part, scores = gates(dot_nt(queries, vk_ref[rows, HEAD_DIM:]), allowed)
        weights = (scores * part).astype(BF16)
        mixed_sum = mixed_sum + dot_nn(weights, vk_ref[rows, :HEAD_DIM])
    center = mixed_sum - jnp.mean(mixed_sum, axis=-1, keepdims=True)
    inverse = lax.rsqrt(jnp.mean(center * center, axis=-1, keepdims=True) + EPSILON)
    normed = center * inverse
    gating = gate_ref[...].astype(F32)
    head = lax.axis_index("h")
    for k, part in enumerate((s0, s1, s2, s3)):
        held[block_rows(head ^ k), HEAD_DIM:] = part[:ROWS]
    upstream = held[:, HEAD_DIM:].astype(F32)
    layer = (normed * gating).astype(BF16)
    grad_normed = upstream * gating
    mixed_ref[...] = (
        (
            grad_normed
            - jnp.mean(grad_normed, axis=-1, keepdims=True)
            - normed * jnp.mean(grad_normed * normed, axis=-1, keepdims=True)
        )
        * inverse
    ).astype(BF16)
    gate_grad_ref[...] = (upstream * normed).astype(BF16)
    held[:, :HEAD_DIM] = layer
    for k, layer_ref in enumerate((l0, l1, l2, l3)):
        layer_ref[...] = held[block_rows(head ^ k), :HEAD_DIM]


def key_gates(keys, key_pos, queries, query_pos, low):
    part, scores = gates(dot_nt(keys, queries), pairs_allowed(key_pos, query_pos, low))
    weights = scores * part
    return weights.astype(BF16), part * (1.0 + scores - weights)


def key_grads(weights, slope, values, queries, grad_mixed):
    grad_scores = (dot_nt(values, grad_mixed) * slope).astype(BF16)
    return dot_nn(weights, grad_mixed), dot_nn(grad_scores, queries)


def query_grad_kernel(
    low_ref, low_rows_ref, s0, s2, s3, s1, mixed_ref, gate_grad_ref, query_ref, q1_ref,
    vk1_ref, vk2_ref, vk0_ref, out_ref, own_ref, picks_ref, weights_ref, slope_ref, done,
):
    low = low_down(low_ref)
    quarter = lax.axis_index("x")
    own_pos = quarter * PART + iota((PART, 1), 0)
    queries = query_ref[...]
    grad_mixed = mixed_ref[...]
    total = jnp.zeros((PART, HEAD_DIM), F32)
    for vk_ref, rows, at in steps_of(
        (vk2_ref, vk1_ref, vk0_ref), (quarter - 2, quarter - 1, quarter)
    ):
        keys = vk_ref[rows, HEAD_DIM:]
        allowed = pairs_allowed(at + iota((1, STEP), 1), own_pos, low)
        part, scores = gates(dot_nt(queries, keys), allowed)
        slope = part * (1.0 + scores - scores * part)
        grad_scores = (dot_nt(grad_mixed, vk_ref[rows, :HEAD_DIM]) * slope).astype(BF16)
        total = total + dot_nn(grad_scores, keys)
    done[0] = gate_grad_ref[...]
    done[1] = (total * SCALE).astype(BF16)
    back_picks((s0, s1, s2, s3), picks_ref)
    pack_back(picks_ref, done, out_ref, 0)
    values, keys = vk0_ref[:, :HEAD_DIM], vk0_ref[:, HEAD_DIM:]
    sums = (0.0, 0.0)
    for part, rows, at in steps_of((query_ref,), (quarter,)):
        weights, slope = key_gates(
            keys, own_pos, part[rows], at + iota((1, STEP), 1), low_rows_ref[0:1, rows]
        )
        terms = key_grads(weights, slope, values, part[rows], mixed_ref[rows])
        sums = tuple(a + b for a, b in zip(sums, terms))
    for n in range(2):
        own_ref[n] = sums[n]
    for n, (part, rows, at) in enumerate(steps_of((q1_ref,), (quarter + 1,))):
        along = PART + n * STEP
        weights_ref[n], slope_ref[n] = key_gates(
            keys, own_pos, part[rows], at + iota((1, STEP), 1),
            low_rows_ref[0:1, along : along + STEP],
        )


def back_picks(sides, picks_ref):
    sublane = iota((N_DP * CHUNK, 2 * ROWS), 0)
    for k, side_ref in enumerate(sides):
        at = both_halves(code_across(side_ref).astype(jnp.int32), 1)
        picks_ref[lax.axis_index("h") ^ k] = jnp.where(sublane == at, 1.0, 0.0).astype(BF16)


def pack_back(picks_ref, done, out_ref, j, finished=lambda c: None):
    for c in range(HEADS):
        rows = slice(c * ROWS, (c + 1) * ROWS)
        both = jnp.concatenate([done[0, rows], done[1, rows]], axis=0)
        out_ref[:, c, :, j * HEAD_DIM : (j + 1) * HEAD_DIM] = (
            dot_nn(picks_ref[c], both).astype(BF16).reshape(N_DP, CHUNK, HEAD_DIM)
        )
        finished(c)


def backward_kernel(
    low_rows_ref, picks_ref, vk_ref, q2_ref, q1_ref, m2_ref, m1_ref,
    own_ref, weights_ref, slope_ref, gq_ref, out_ref, done, packed, sems,
):
    packed[:, :, :, :HEAD_DIM] = gq_ref[...]
    quarter = lax.axis_index("x")
    own_pos = quarter * PART + iota((PART, 1), 0)
    values, keys = vk_ref[:, :HEAD_DIM], vk_ref[:, HEAD_DIM:]
    sums = (own_ref[0], own_ref[1])
    later = steps_of(((q1_ref, m1_ref), (q2_ref, m2_ref)), (quarter + 1, quarter + 2))
    for n, ((part, mixed), rows, at) in enumerate(later):
        along = PART + n * STEP
        if n < PART // STEP:
            weights, slope = weights_ref[n], slope_ref[n]
        else:
            weights, slope = key_gates(
                keys, own_pos, part[rows], at + iota((1, STEP), 1),
                low_rows_ref[0:1, along : along + STEP],
            )
        terms = key_grads(weights, slope, values, part[rows], mixed[rows])
        sums = tuple(a + b for a, b in zip(sums, terms))
    done[0] = sums[0].astype(BF16)
    done[1] = (sums[1] * SCALE).astype(BF16)
    stores = []

    def send(c):
        stores.append(pltpu.make_async_copy(packed.at[:, c], out_ref.at[:, c], sems.at[c]))
        stores[-1].start()

    pack_back(picks_ref, done, packed, 1, send)
    for store in stores:
        store.wait()


def finish_kernel(
    home_ref, l0, l2, l3, l1, back_ref, grad_ref, out_ref, grads, sems
):
    stores = []
    for k, layer_ref in enumerate((l0, l1, l2, l3)):
        columns = head_columns(lax.axis_index("h") ^ k)
        stores.append(pltpu.make_async_copy(layer_ref, out_ref.at[:, columns], sems.at[k]))
        stores[-1].start()
    pick = home_ref[...]
    for h in range(HEADS):
        chunks = back_ref[:, h].reshape(N_DP * CHUNK, 2 * HEAD_DIM)
        moved = dot_nn(pick, chunks).astype(BF16)
        for half in range(2):
            for j in range(2):
                block = 2 * half + j
                at = (block * HEADS + h) * HEAD_DIM
                columns = slice(at, at + HEAD_DIM)
                grads[:, columns] = moved[
                    half * ROWS : (half + 1) * ROWS, j * HEAD_DIM : (j + 1) * HEAD_DIM
                ]
                stores.append(
                    pltpu.make_async_copy(
                        grads.at[:, columns], grad_ref.at[:, columns], sems.at[HEADS + 4 * h + block]
                    )
                )
                stores[-1].start()
    for store in stores:
        store.wait()


def route(chunks):
    flat = chunks.reshape(N_DP * HEADS * CHUNK, 2 * HEAD_DIM)
    moved = lax.all_to_all(flat, ("dp", "h"), 0, 0, tiled=True)
    return moved.reshape(chunks.shape)


def from_quarter(array, by):
    pairs = [(i, i - by) for i in range(N_X) if 0 <= i - by < N_X]
    return lax.ppermute(array, "x", pairs)


def swap_heads(pieces):
    return [pieces[0]] + [
        lax.ppermute(pieces[k], "h", [(i, i ^ k) for i in range(HEADS)]) for k in (2, 3, 1)
    ]


def body(projected, destination, lengths, grad_out):
    mapping = destination.reshape(N_DP, ROWS)
    chunked = shape(N_DP, HEADS, CHUNK, 2 * HEAD_DIM)
    half_chunked = shape(N_DP, HEADS, CHUNK, HEAD_DIM)
    head_part = shape(PART, HEAD_DIM)
    pieces = [shape(ROWS, HEAD_DIM)] * HEADS
    dma = pltpu.SemaphoreType.DMA
    (packed,) = call(
        pack_kernel, [chunked], (mapping, projected),
        scratch=[
            pltpu.VMEM(projected.shape, BF16), pltpu.VMEM(chunked.shape, BF16), dma, dma((2,)),
        ],
        flops=2 * 256 * 128 * 2048, nbytes=3 << 19,
        hbm_in=(1,), hbm_out=True, limit=62 * 1024 * 1024,
    )
    side_out = call(
        side_kernel, [shape(ROWS + CHUNK, HEAD_DIM)] * HEADS, (mapping, grad_out),
        nbytes=3 << 17,
    )
    home, low, low_rows = call(
        plan_kernel,
        [
            shape(2 * ROWS, N_DP * CHUNK), shape(PART, ROWS, dtype=jnp.int32),
            shape(8, (REACH + 1) * PART, dtype=jnp.int32),
        ],
        (lengths, mapping, side_out[0]), smem=(0,), nbytes=3 << 17,
    )
    side = swap_heads(side_out)
    arrived = route(packed)
    gate, queries, vk = call(
        unpack_kernel, [head_part, head_part, shape(PART, 2 * HEAD_DIM)], (*side, arrived),
        flops=1 << 28, nbytes=2 << 20,
    )
    vk_parts = (from_quarter(vk, -1), from_quarter(vk, -2), vk)
    query_parts = (from_quarter(queries, 2), from_quarter(queries, 1))
    held = pltpu.VMEM((PART, 2 * HEAD_DIM), BF16)
    done = pltpu.VMEM((2, PART, HEAD_DIM), BF16)
    mixed, gate_grad, *layer = call(
        forward_kernel, [head_part, head_part, *pieces],
        (low, *side, gate, queries, *vk_parts),
        scratch=[held], flops=1 << 29, nbytes=2 << 20,
    )
    mixed_parts = (from_quarter(mixed, 2), from_quarter(mixed, 1))
    layer_home = swap_heads(layer)
    gq_back, own, picks, weights, slopes = call(
        query_grad_kernel,
        [half_chunked, shape(2, PART, HEAD_DIM, dtype=F32), shape(HEADS, N_DP * CHUNK, 2 * ROWS),
         shape(PART // STEP, PART, STEP), shape(PART // STEP, PART, STEP, dtype=F32)],
        (low, low_rows, *side, mixed, gate_grad, queries, query_parts[1], *vk_parts),
        scratch=[done], flops=1 << 29, nbytes=2 << 20,
    )
    (back,) = call(
        backward_kernel, [chunked],
        (low_rows, picks, vk, *query_parts, *mixed_parts, own, weights, slopes, gq_back),
        scratch=[done, pltpu.VMEM(chunked.shape, BF16), dma((HEADS,))],
        flops=1 << 30, nbytes=3 << 20, hbm_out=True,
    )
    returned = route(back)
    grad_projected, layer_output = call(
        finish_kernel, [shape(ROWS, 4 * HEADS * HEAD_DIM), shape(ROWS, HEADS * HEAD_DIM)],
        (home, *layer_home, returned),
        scratch=[pltpu.VMEM(projected.shape, BF16), dma((5 * HEADS,))],
        flops=1 << 28, nbytes=2 << 20, hbm_out=True,
    )
    return (layer_output, grad_projected)


def solution(mesh):
    fine = Mesh(mesh.devices.reshape(N_DP, N_X, HEADS), ("dp", "x", "h"))
    rows = P(("dp", "x", "h"), None)
    in_specs = (rows, P(("x", "h"), None), P("dp", None), rows)
    return jax.shard_map(
        body, mesh=fine, in_specs=in_specs, out_specs=(rows, rows), check_vma=False
    )
```
